32 devices in a mesh: pipe: 4 (over y, x), ctx: 8 (over z, core).
Axes of the slice: x: 2, y: 2, z: 4, core: 2. Of those that a mesh axis runs over, the one named last changes fastest.
Arguments:
- x_in: bfloat16 [4, 512, 8192], P('pipe', 'ctx'), may hold values from -6 to 6
- z_in: bfloat16 [4, 512, 8192], P('pipe', 'ctx'), may hold values from -6 to 6
- bc_in: bfloat16 [4, 512, 1024], P('pipe', 'ctx'), may hold values from -6 to 6
- dt_raw: bfloat16 [4, 512, 128], P('pipe', 'ctx'), may hold values from -3.2 to 3.2
- a_log: float32 [4, 128], P('pipe'), may hold values from -12 to 3
- dt_bias: float32 [4, 128], P('pipe'), may hold values from -3.8 to -3
- d_skip: float32 [4, 128], P('pipe'), may hold values from 0.5 to 1.5
- conv_x: bfloat16 [4, 4, 8192], P('pipe'), may hold values from -3 to 3
- conv_bc: bfloat16 [4, 4, 1024], P('pipe'), may hold values from -3 to 3
- norm_gain: float32 [4, 8192], P('pipe'), may hold values from 0.5 to 1.5
- seg_ids: int32 [4, 512], P('pipe', 'ctx'), may hold values from 0 to 3, never falling along the last dimension, each value on 1 to 256 neighbouring positions
- query: bfloat16 [4, 512, 2048], P('pipe', 'ctx'), may hold values from -192 to 192
- keys: bfloat16 [4, 512, 256], P('pipe', 'ctx'), may hold values from -6 to 6
- values: bfloat16 [4, 512, 256], P('pipe', 'ctx'), may hold values from -6 to 6
Outputs:
- mamba_out: bfloat16 [4, 512, 8192], P('pipe', 'ctx')
- handoff: bfloat16 [4, 512, 2048], P('pipe', 'ctx')
The draws below stay inside these ranges and needn't reach their ends.
Inputs may be any that keep to these rules, and one draw needn't show every extreme that they name: `seg_ids`: segment numbers never fall along a section's sequence; no segment is longer than 256 positions, and one has exactly that many.
All inputs are finite; a program needn't handle non-finite values.
Results may differ from the reference program's by a relative error of at most 0.0044.
The reference program's roundings to bfloat16 on the way count: a program that leaves them out, or rounds other values in their place, can miss the bound.
Values may be sent and summed in bfloat16 or wider, within the bound.
No kernel may reach another device: no remote copies, remote signals or barrier semaphores. Data moves between devices by JAX's collectives and lax.ppermute only.
A program may use at most 128 MiB of HBM per device.

```python
import math
import jax
import jax.numpy as jnp
import numpy as np
from jax import lax

H = 128
P_SIZE = 64
N = 128
G = 4
KC = 4
AH = 32
KVH = 4
HD = 64
SEGS = 4
TOK_DEV = 64
SECT = 4
SEQ = 512
BLK = 256


def attention_pair(key):
    base = jax.random.fold_in(key, 41)
    key_seed, query_seed = jax.random.split(base)
    ratio = AH // KVH
    grouped_key_rows = jnp.clip(jax.random.normal(key_seed, (SECT, SEQ, KVH, HD), jnp.float32), -6.0, 6.0)
    queries = 2.5 * jnp.clip(jax.random.normal(query_seed, (SECT, SEQ, KVH, ratio, HD), jnp.float32), -6.0, 6.0)
    return (queries.reshape(SECT, SEQ, AH * HD), grouped_key_rows.reshape(SECT, SEQ, KVH * HD))


def draw_query(key, part):
    return attention_pair(key)[0].astype(jnp.bfloat16)


def draw_keys(key, part):
    return attention_pair(key)[1].astype(jnp.bfloat16)


def draw_a_log(key, part):
    pick_seed, level_seed = jax.random.split(jax.random.fold_in(key, 3))
    share = 0.5
    fast = jax.random.uniform(pick_seed, (SECT, H), jnp.float32) < share
    level = jax.random.uniform(level_seed, (SECT, H), jnp.float32)
    fast_rate = math.log(1.0 / 50.0) + level * math.log(50.0 / 30.0)
    slow_rate = math.log(0.1) + level * math.log(6.0) - math.log(SEQ)
    return jnp.where(fast, fast_rate, slow_rate) - math.log(0.033)


def draw_dt_raw(key, part):
    noise_seed, offset_seed = jax.random.split(jax.random.fold_in(key, 5))
    noise = 0.4 * jnp.clip(jax.random.normal(noise_seed, (SECT, SEQ, H), jnp.float32), -6.0, 6.0)
    offsets = jax.random.uniform(offset_seed, (SECT, SEQ // TOK_DEV, H), jnp.float32, -0.7, 0.7)
    return (noise + jnp.repeat(offsets, TOK_DEV, axis=1)).astype(jnp.bfloat16)


def block_scale(key, dims, cuts, smallest, high):
    def one(dim, blocks):
        heights = jax.random.uniform(jax.random.fold_in(jax.random.fold_in(key, 6), dim), (blocks,), jnp.float32, smallest / len(cuts), high / len(cuts))
        return jnp.repeat(jnp.exp(heights), dims[dim] // blocks).reshape((-1,) + (1,) * (len(dims) - dim - 1))

    factor_of = one(*cuts[0])
    for cut in cuts[1:]:
        factor_of = factor_of * one(*cut)
    return factor_of


def split_up(count, total, reach, lean):
    portions = [(1 << 20) // math.isqrt(grade ** lean) + 1 for grade in range(2, count + 1)]
    rest, given = total - reach - (count - 1), [1] * (count - 1)
    while rest > 0:
        candidates = [i for i in range(count - 1) if given[i] < reach]
        pool, remaining = sum([portions[i] for i in candidates]), rest
        for i in candidates:
            addition = min(reach - given[i], max(1, remaining * portions[i] // pool), rest)
            given[i] = given[i] + addition
            rest = rest - addition
    return np.array([reach] + given)


def uneven(own_key, count, total, bound, slope):
    if count == 2:
        one = jax.random.randint(own_key, (), max(1, total - bound), min(bound, total - 1) + 1)
        return jnp.stack([one, total - one])
    lengths = jnp.asarray(split_up(count, total, bound, slope), jnp.int32)
    couples = (count - 1) // 2
    giver, taker = lengths[1:1 + 2 * couples:2], lengths[2:2 + 2 * couples:2]
    room = jnp.minimum(giver - 1, bound - taker)
    passed = jax.random.randint(jax.random.fold_in(own_key, 1), (couples,), 0, 1 << 20) % (room + 1)
    lengths = lengths.at[1:1 + 2 * couples:2].set(giver - passed).at[2:2 + 2 * couples:2].set(taker + passed)
    return lengths[jax.random.permutation(jax.random.fold_in(own_key, 2), count)]


def scatter_about(rng, dims, scale, reach, shards=(), kind=jnp.bfloat16):
    values = jax.random.normal(rng, dims, jnp.float32) * scale
    if len(shards) > 0:
        values = block_scale(rng, dims, shards, -0.22, 0.18) * values
    return jnp.clip(values, min=-reach, max=reach).astype(kind)


def setup_inputs(seed: int = 0) -> dict:
    arg_keys = jax.random.split(jax.random.key(seed), 15)
    return {
        "x_in": scatter_about(arg_keys[0], (SECT, SEQ, H * P_SIZE), 1.0, 6.0, ((0, 4), (1, 8))),
        "z_in": scatter_about(arg_keys[1], (SECT, SEQ, H * P_SIZE), 1.0, 6.0, ((0, 4), (1, 8))),
        "bc_in": scatter_about(arg_keys[2], (SECT, SEQ, 2 * G * N), 1.0, 6.0, ((0, 4), (1, 8))),
        "dt_raw": draw_dt_raw(jax.random.fold_in(arg_keys[14], 71), 0),
        "a_log": draw_a_log(jax.random.fold_in(arg_keys[14], 71), 0),
        "dt_bias": jnp.clip(-3.8 + 0.79999995 * jax.random.uniform(arg_keys[5], (SECT, H), jnp.float32) ** block_scale(arg_keys[5], (SECT, H), ((0, 4),), -0.2, 0.2), -3.8, -3.0),
        "d_skip": jnp.clip(0.5 + 1.0 * jax.random.uniform(arg_keys[6], (SECT, H), jnp.float32) ** block_scale(arg_keys[6], (SECT, H), ((0, 4),), -0.2, 0.2), 0.5, 1.5),
        "conv_x": scatter_about(arg_keys[7], (SECT, KC, H * P_SIZE), KC ** -0.5, 3.0, ((0, 4),)),
        "conv_bc": scatter_about(arg_keys[8], (SECT, KC, 2 * G * N), KC ** -0.5, 3.0, ((0, 4),)),
        "norm_gain": jnp.clip(1.0 + 0.1 * jax.random.normal(arg_keys[9], (SECT, H * P_SIZE), jnp.float32), 0.5, 1.5),
        "seg_ids": jax.vmap(lambda own: jnp.searchsorted(jnp.cumsum(uneven(own, SEGS, SEQ, SEQ // 2, 2)), jnp.arange(SEQ), side="right"))(jax.random.split(arg_keys[10], SECT)).reshape((SECT, SEQ)).astype(jnp.int32),
        "query": draw_query(jax.random.fold_in(arg_keys[14], 71), 0),
        "keys": draw_keys(jax.random.fold_in(arg_keys[14], 71), 0),
        "values": scatter_about(arg_keys[13], (SECT, SEQ, KVH * HD), 1.0, 6.0, ((0, 4), (1, 8))),
    }


norm_eps = 1e-05

def causal_taps(inputs, weights, ids):
    lag = KC - 1
    length = inputs.shape[0]
    padded = jnp.concatenate([jnp.zeros((lag,) + inputs.shape[1:], inputs.dtype), inputs], axis=0)
    padded_ids = jnp.concatenate([jnp.full((lag,), -1, jnp.int32), ids.astype(jnp.int32)])
    layout = (length,) + (1,) * (inputs.ndim - 1)
    summed = jnp.zeros(inputs.shape, jnp.float32)
    for tap in range(lag + 1):
        same = (padded_ids[tap:tap + length] == ids).reshape(layout)
        summed = summed + jnp.where(same, weights[tap].astype(jnp.float32) * padded[tap:tap + length].astype(jnp.float32), 0.0)
    return jax.nn.silu(summed).astype(jnp.bfloat16)

def state_space(x_conv, bc_conv, step_size, rates, skip, ids):
    length, local_heads, head_dim = x_conv.shape
    states = bc_conv.shape[2] // 2
    span = BLK
    blocks = length // span
    lower = jnp.arange(span)[:, None] >= jnp.arange(span)[None, :]
    score_peak = lax.Precision.HIGHEST

    def advance(carry, item):
        memory, last_id = carry
        x_block, bc_block, step_block, id_block = item
        b_part = bc_block[:, :, :states].astype(jnp.float32)
        c_part = bc_block[:, :, states:].astype(jnp.float32)
        logs = jnp.cumsum(step_block * rates[None, :], axis=0)
        allowed = lower & (id_block[:, None] == id_block[None, :])
        gaps = logs[:, None, :] - logs[None, :, :]
        weights = jnp.where(allowed[:, :, None], jnp.exp(jnp.minimum(gaps, 0.0)), 0.0) * step_block[None, :, :]
        inner = jnp.einsum('thn,shn->tsh', c_part, b_part, precision=score_peak)
        mixing = (inner * weights).astype(jnp.bfloat16)
        local_part = jnp.einsum('tsh,shp->thp', mixing.astype(jnp.float32), x_block.astype(jnp.float32), precision=score_peak)
        keep = jnp.where((id_block == last_id)[:, None], jnp.exp(logs), 0.0)
        carried = jnp.einsum('thn,hpn->thp', c_part, memory, precision=score_peak) * keep[:, :, None]
        result = local_part + carried + skip[None, :, None] * x_block.astype(jnp.float32)
        tail = logs[span - 1]
        writes = jnp.where((id_block == id_block[span - 1])[:, None], jnp.exp(tail[None, :] - logs), 0.0) * step_block
        scaled = (x_block.astype(jnp.float32) * writes[:, :, None]).astype(jnp.bfloat16)
        added = jnp.einsum('shp,shn->hpn', scaled.astype(jnp.float32), b_part, precision=score_peak)
        kept = jnp.where(id_block[span - 1] == last_id, jnp.exp(tail), 0.0)
        memory = memory * kept[:, None, None] + added
        return ((memory, id_block[span - 1]), result)
    start = (jnp.zeros((local_heads, head_dim, states), jnp.float32), jnp.array(-1, jnp.int32))
    items = (x_conv.reshape(blocks, span, local_heads, head_dim), bc_conv.reshape(blocks, span, local_heads, 2 * states), step_size.reshape(blocks, span, local_heads), ids.reshape(blocks, span))
    _, outputs = lax.scan(advance, start, items)
    return outputs.reshape(length, local_heads, head_dim)

def mamba_section(x_sec, z_sec, bc_sec, raw_sec, alog_sec, bias_sec, skip_sec, convx_sec, convbc_sec, gain_sec, ids):
    x_conv = causal_taps(x_sec, convx_sec, ids).reshape(SEQ, H, P_SIZE)
    bc_conv = causal_taps(bc_sec, convbc_sec, ids).reshape(SEQ, 2, G, N)
    step_size = jax.nn.softplus(raw_sec.astype(jnp.float32) + bias_sec[None, :])
    decay_rate = -jnp.exp(alog_sec)

    def one_head(head):
        group = head // (H // G)
        x_head = lax.dynamic_index_in_dim(x_conv, head, 1, keepdims=True)
        bc_head = lax.dynamic_index_in_dim(bc_conv, group, 2, keepdims=False).reshape(SEQ, 1, 2 * N)
        step_head = lax.dynamic_index_in_dim(step_size, head, 1, keepdims=True)
        rate_head = lax.dynamic_index_in_dim(decay_rate, head, 0, keepdims=True)
        skip_head = lax.dynamic_index_in_dim(skip_sec, head, 0, keepdims=True)
        return state_space(x_head, bc_head, step_head, rate_head, skip_head, ids)[:, 0, :]
    attention_mixture = lax.map(one_head, jnp.arange(H, dtype=jnp.int32))
    attention_mixture = jnp.transpose(attention_mixture, (1, 0, 2)).astype(jnp.bfloat16).reshape(SEQ, H * P_SIZE)
    gated = attention_mixture.astype(jnp.float32) * jax.nn.silu(z_sec.astype(jnp.float32))
    grouped = gated.reshape(SEQ, G, H * P_SIZE // G)
    factor = lax.rsqrt(lax.optimization_barrier(jnp.mean(grouped * grouped, axis=-1, keepdims=True)) + norm_eps)
    return ((grouped * factor).reshape(SEQ, H * P_SIZE) * gain_sec[None, :]).astype(jnp.bfloat16)

def attention_section(q_sec, k_sec, v_sec, ids):
    ratio = AH // KVH
    queries = q_sec.reshape(SEQ, KVH, ratio, HD).astype(jnp.float32)
    grouped_key_rows = k_sec.reshape(SEQ, KVH, HD).astype(jnp.float32)
    grouped_value_rows = v_sec.reshape(SEQ, KVH, HD).astype(jnp.float32)
    rows = math.gcd(SEQ, 128)
    places = jnp.arange(SEQ)
    logit_scale = 1.0 / math.sqrt(HD)
    score_peak = lax.Precision.HIGHEST

    def one_block(order):
        first = order * rows
        query_tile_rows = lax.dynamic_slice_in_dim(queries, first, rows)
        query_ids = lax.dynamic_slice_in_dim(ids, first, rows)
        query_pos = first + jnp.arange(rows)
        attention_logits = jnp.einsum('cofa,moa->ofcm', query_tile_rows, grouped_key_rows, precision=score_peak) * logit_scale
        allowed = (query_pos[:, None] >= places[None, :]) & (query_ids[:, None] == ids[None, :])
        masked = jnp.where(allowed, attention_logits, -1e+30)
        top = lax.optimization_barrier(jnp.max(masked, axis=-1, keepdims=True))
        weight = jnp.where(allowed, jnp.exp(masked - top), 0.0)
        totals = lax.optimization_barrier(jnp.sum(weight, axis=-1))
        softmax_weights = weight.astype(jnp.bfloat16)
        attention_mixture = jnp.einsum('hxbp,phi->hxbi', softmax_weights.astype(jnp.float32), grouped_value_rows, precision=score_peak)
        result = attention_mixture / totals[..., None]
        return jnp.transpose(result, (2, 0, 1, 3)).reshape(rows, AH * HD)
    blocks = lax.map(one_block, jnp.arange(SEQ // rows, dtype=jnp.int32))
    return blocks.reshape(SEQ, AH * HD).astype(jnp.bfloat16)

def reference(x_in, z_in, bc_in, dt_raw, a_log, dt_bias, d_skip, conv_x, conv_bc, norm_gain, seg_ids, query, keys, values):
    mamba_parts = []
    attended = []
    for section in range(SECT):
        ids = seg_ids[section].astype(jnp.int32)
        mamba_parts.append(mamba_section(x_in[section], z_in[section], bc_in[section], dt_raw[section], a_log[section], dt_bias[section], d_skip[section], conv_x[section], conv_bc[section], norm_gain[section], ids))
        attended.append(attention_section(query[section], keys[section], values[section], ids))
    mamba_out = jnp.stack(mamba_parts)
    handoff = jnp.roll(jnp.stack(attended), 1, axis=0)
    return (mamba_out, handoff)
```

```python
import functools
import math

import jax
import jax.numpy as jnp
from jax import lax
from jax.experimental import pallas as pl
from jax.experimental.pallas import tpu as pltpu
from jax.sharding import PartitionSpec as P

G = 4
AH = 32
KVH = 4
HD = 64
BLK = 256
LANES = 128
LOCAL_HEADS = 32
CHUNKS = 2

norm_eps = 1e-05
bf16 = jnp.bfloat16
f32 = jnp.float32


def shifted(value, axis, steps):
    count = lax.axis_size(axis)
    return lax.ppermute(value, axis, [(i, i + steps) for i in range(count - steps)])


def crossed(value, axis, mask):
    count = lax.axis_size(axis)
    return lax.ppermute(value, axis, [(i, i ^ mask) for i in range(count)])


def from_behind(value, axis, steps):
    count = lax.axis_size(axis)
    return lax.ppermute(value, axis, [(i, (i + steps) % count) for i in range(count)])


def iota(shape, dim):
    return lax.broadcasted_iota(jnp.int32, shape, dim)


def call(body, outs, scratch=(), flops=0, bytes_accessed=0):
    return pl.pallas_call(
        body,
        out_shape=outs,
        scratch_shapes=list(scratch),
        compiler_params=pltpu.CompilerParams(vmem_limit_bytes=48 * 2**20),
        cost_estimate=pl.CostEstimate(
            flops=flops, bytes_accessed=bytes_accessed, transcendentals=0
        ),
    )


def pack_body(share, chunk, x_ref, bc_ref, dt_ref, ids_ref, k_ref, v_ref, *outs):
    me = lax.rem(lax.axis_index("ctx"), share)
    rows, width = x_ref.shape
    piece = width // share
    states = bc_ref.shape[1] // (2 * G)
    a_refs, b_refs, kv_refs = outs[:share], outs[share : 2 * share], outs[2 * share :]
    number = ids_ref[...].astype(f32) + 1.0
    square = iota((rows, rows), 0) == iota((rows, rows), 1)
    column = jnp.sum(
        jnp.where(square, jnp.broadcast_to(number, (rows, rows)), 0.0), axis=1, keepdims=True
    )
    spread_ids = jnp.broadcast_to(column, (rows, LANES)).astype(bf16)
    steps = dt_ref[...]
    for m in range(share):
        s = me ^ m
        base = pl.multiple_of(s * piece, LANES)
        b_at = pl.multiple_of(s * states, LANES)
        c_at = pl.multiple_of(G * states + s * states, LANES)
        a_refs[m][:, :chunk] = x_ref[:, pl.ds(base, chunk)]
        a_refs[m][:, chunk : chunk + states] = bc_ref[:, pl.ds(b_at, states)]
        a_refs[m][:, chunk + states : chunk + 2 * states] = bc_ref[:, pl.ds(c_at, states)]
        a_refs[m][:, chunk + 2 * states : chunk + 3 * states] = steps
        a_refs[m][:, chunk + 3 * states :] = spread_ids
        b_refs[m][...] = x_ref[:, pl.ds(pl.multiple_of(base + chunk, LANES), chunk)]
    wide = 4 * LANES
    lane = iota((rows, wide), 1)
    row = iota((rows, wide), 0)
    which = iota((16, wide), 0)
    for r, kv in enumerate(kv_refs):
        kv[:rows, : wide // 2] = k_ref[...]
        kv[:rows, wide // 2 :] = v_ref[...]
        id_row = jnp.sum(jnp.where(lane == row + rows * r, column, 0.0), axis=0, keepdims=True)
        block = jnp.where(which == 15, id_row, 0.0)
        if r > 0:
            s = lax.rem(me + r, share)
            base = pl.multiple_of(s * piece, LANES)
            b_at = pl.multiple_of(s * states, LANES)
            c_at = pl.multiple_of(G * states + s * states, LANES)
            last = pl.ds(rows - 16, 16)
            parts = [
                x_ref[last, pl.ds(pl.multiple_of(base + p * wide, LANES), wide)].astype(f32)
                for p in range(piece // wide)
            ]
            parts.append(
                jnp.concatenate(
                    [
                        bc_ref[last, pl.ds(b_at, states)],
                        bc_ref[last, pl.ds(c_at, states)],
                        dt_ref[last, :],
                        spread_ids[rows - 16 :],
                    ],
                    axis=1,
                ).astype(f32)
            )
            for i in range(3):
                for p, part in enumerate(parts):
                    block = jnp.where(which == 5 * i + p, part[13 + i : 14 + i, :], block)
        kv[rows:, :] = block.astype(bf16)


def place_halo(scratch, halos, pieces, me):
    rows = halos[0].shape[0]
    picked = halos[0][rows - 16 :, :].astype(f32)
    for r in range(1, len(halos)):
        picked = jnp.where(me == r, halos[r][rows - 16 :, :].astype(f32), picked)
    for at, p in enumerate(pieces):
        wide = picked.shape[1]
        which = iota((8, wide), 0)
        block = jnp.zeros((8, wide), f32)
        for i in range(3):
            block = jnp.where(which == 5 + i, picked[5 * i + p : 5 * i + p + 1, :], block)
        scratch[0:8, at * wide : (at + 1) * wide] = block


def conv_strip(src, columns, masks, taps):
    length = masks.shape[1]
    total = None
    for tap in range(4):
        term = taps[tap] * src[5 + tap : 5 + tap + length, columns]
        if tap < 3:
            term = term * masks[tap]
        total = term if total is None else total + term
    return (total * jax.nn.sigmoid(total)).astype(bf16)


def set_masks(masks, ids):
    length = masks.shape[1]
    own = ids[8 : 8 + length, :]
    for tap in range(3):
        masks[tap] = jnp.where(ids[5 + tap : 5 + tap + length, :] == own, 1.0, 0.0)


def one_hot(first, chunk):
    lane = iota((LANES, chunk), 0)
    head = iota((LANES, chunk), 1) // HD + first
    return jnp.where((lane % LOCAL_HEADS == head) & (lane < 3 * LOCAL_HEADS), 1.0, 0.0).astype(bf16)


def three_parts(value):
    lane = iota(value.shape, 1)
    high = value.astype(bf16).astype(f32)
    rest = value - high
    middle = rest.astype(bf16).astype(f32)
    low = rest - middle
    packed = jnp.where(
        lane < LOCAL_HEADS,
        high,
        jnp.where(
            lane < 2 * LOCAL_HEADS,
            pltpu.roll(middle, LOCAL_HEADS, 1),
            jnp.where(lane < 3 * LOCAL_HEADS, pltpu.roll(low, 2 * LOCAL_HEADS, 1), 0.0),
        ),
    )
    return packed.astype(bf16)


def conv_x_and_state(xs, masks, conv_ref, base, bcc, writes, first, xc_ref, state_ref):
    chunk = xc_ref.shape[1]
    for c in range(chunk // LANES):
        columns = slice(c * LANES, (c + 1) * LANES)
        weights = conv_ref[:, pl.ds(pl.multiple_of(base + c * LANES, LANES), LANES)].astype(f32)
        taps = [weights[t : t + 1, :] for t in range(4)]
        xc_ref[:, columns] = conv_strip(xs, columns, masks, taps)
    factors = jnp.dot(writes, one_hot(first, chunk), preferred_element_type=f32)
    scaled = (xc_ref[...].astype(f32) * factors).astype(bf16)
    state = lax.dot_general(bcc, scaled, (((0,), (0,)), ((), ())), preferred_element_type=f32)
    state_ref[...] = state.astype(state_ref.dtype)


def first_body(share, *refs):
    halos, pieces = refs[:share], refs[share : 2 * share]
    convx, convbc, bias, alog = refs[2 * share : 2 * share + 4]
    xc_o, bcc_o, state_o, ids_o, cum_o, step_o, writes_o, keep_o, xs, bs, masks = refs[
        2 * share + 4 :
    ]
    me = lax.rem(lax.axis_index("ctx"), share)
    chunk = xc_o.shape[1]
    rows = pieces[0].shape[0]
    length = rows * share
    per_block = 4 * LANES
    place_halo(xs, halos, list(range(chunk // per_block)), me)
    place_halo(bs, halos, [4], me)
    for m in range(share):
        at = pl.multiple_of(8 + rows * (me ^ m), 8)
        xs[pl.ds(at, rows), :] = pieces[m][:, :chunk].astype(f32)
        bs[pl.ds(at, rows), :] = pieces[m][:, chunk:].astype(f32)
    ids_o[...] = bs[:, 3 * LANES : 4 * LANES]
    set_masks(masks, ids_o)
    for half in range(2):
        columns = slice(half * LANES, (half + 1) * LANES)
        at = pl.multiple_of(half * G * LANES + me * LANES, LANES)
        weights = convbc[:, pl.ds(at, LANES)].astype(f32)
        taps = [weights[t : t + 1, :] for t in range(4)]
        bcc_o[:, columns] = conv_strip(bs, columns, masks, taps)
    raw = bs[8:, 2 * LANES : 3 * LANES] + bias[...]
    step = jnp.maximum(raw, 0.0) + jnp.log1p(jnp.exp(-jnp.abs(raw)))
    total = step * (-jnp.exp(alog[...]))
    row = iota((length, LANES), 0)
    reach = 1
    while reach < length:
        total = total + jnp.where(row >= reach, pltpu.roll(total, reach, 0), 0.0)
        reach *= 2
    turn = lax.rem(LANES - LOCAL_HEADS * me, LANES)
    total = pltpu.roll(total, turn, 1)
    step = pltpu.roll(step, turn, 1)
    own = ids_o[8:, :]
    last = length - 1
    writes = (
        jnp.where(own == own[last : last + 1, :], jnp.exp(total[last : last + 1, :] - total), 0.0)
        * step
    )
    cum_o[...] = total
    step_o[...] = step
    keep_o[...] = jnp.where(own == ids_o[7:8, :], jnp.exp(total), 0.0)
    packed = three_parts(writes)
    writes_o[...] = packed
    base = me * (chunk * CHUNKS)
    conv_x_and_state(xs, masks, convx, base, bcc_o[:, :LANES], packed, 0, xc_o, state_o)


def second_body(share, *refs):
    halos, pieces = refs[:share], refs[share : 2 * share]
    convx, bcc, ids, writes, xc_o, state_o, xs, masks = refs[2 * share :]
    me = lax.rem(lax.axis_index("ctx"), share)
    chunk = xc_o.shape[1]
    rows = pieces[0].shape[0]
    per_block = 4 * LANES
    blocks = chunk // per_block
    place_halo(xs, halos, list(range(blocks, 2 * blocks)), me)
    for m in range(share):
        at = pl.multiple_of(8 + rows * (me ^ m), 8)
        xs[pl.ds(at, rows), :] = pieces[m][...].astype(f32)
    set_masks(masks, ids)
    base = me * (chunk * CHUNKS) + chunk
    conv_x_and_state(
        xs, masks, convx, base, bcc[:, :LANES], writes[...], chunk // HD, xc_o, state_o
    )


def mixing_body(share, *refs):
    xcs, (bcc, ids, cum, step, skip) = refs[:CHUNKS], refs[CHUNKS : CHUNKS + 5]
    outs = refs[CHUNKS + 5 :]
    me = lax.rem(lax.axis_index("ctx"), share)
    length, chunk = xcs[0].shape
    half = length // 2
    inner = lax.dot_general(
        bcc[:, LANES:], bcc[:, :LANES], (((1,), (1,)), ((), ())), preferred_element_type=f32
    )
    own = ids[8:, :]
    across = own.T[0:1, :]
    own_wide = jnp.concatenate([own, own], axis=1)
    allowed = (iota((length, length), 0) >= iota((length, length), 1)) & (own_wide == across)
    inner = jnp.where(allowed, inner, 0.0)
    cums = cum[...]
    cum_rows = cums.T
    step_rows = step[...].T
    turn = lax.rem(LANES - LOCAL_HEADS * me, LANES)
    gains = three_parts(pltpu.roll(jnp.broadcast_to(skip[...], (8, LANES)), turn, 1))
    even = iota((half, LANES), 1) < HD
    for c in range(CHUNKS):
        first = c * (chunk // HD)
        spread = jnp.dot(gains, one_hot(first, chunk), preferred_element_type=f32)[0:1, :]
        for pair in range(chunk // LANES):
            columns = slice(pair * LANES, (pair + 1) * LANES)
            x_pair = xcs[c][:, columns]
            upper, lower = [], []
            for side in range(2):
                h = first + 2 * pair + side
                fade = cum_rows[h : h + 1, :]
                size = step_rows[h : h + 1, :]
                top = (
                    inner[:half, :half]
                    * (jnp.exp(jnp.minimum(cums[:half, h : h + 1] - fade[:, :half], 0.0)) * size[:, :half])
                ).astype(bf16)
                low = (
                    inner[half:, :]
                    * (jnp.exp(jnp.minimum(cums[half:, h : h + 1] - fade, 0.0)) * size)
                ).astype(bf16)
                upper.append(jnp.dot(top, x_pair[:half, :], preferred_element_type=f32))
                lower.append(jnp.dot(low, x_pair, preferred_element_type=f32))
            gain = spread[:, columns]
            outs[c][:half, columns] = (
                jnp.where(even, upper[0], upper[1]) + gain * x_pair[:half, :].astype(f32)
            )
            outs[c][half:, columns] = (
                jnp.where(even, lower[0], lower[1]) + gain * x_pair[half:, :].astype(f32)
            )


def finish_body(share, first, state, bcc, keep, local, *outs):
    me = lax.rem(lax.axis_index("ctx"), share)
    chunk = local.shape[1]
    rows = outs[0].shape[0]
    carried = jnp.dot(bcc[:, LANES:], state[...], preferred_element_type=f32)
    factors = jnp.dot(three_parts(keep[...]), one_hot(first, chunk), preferred_element_type=f32)
    local[...] = local[...] + carried * factors
    for m in range(share):
        at = pl.multiple_of(rows * (me ^ m), rows)
        outs[m][...] = local[pl.ds(at, rows), :].astype(bf16)


def finish_kernel(share, first, state, bcc, keep, local_in, *rest):
    outs, total = rest[:share], rest[share]
    total[...] = local_in[...]
    finish_body(share, first, state, bcc, keep, total, *outs)


def norm_body(share, *refs):
    firsts, seconds = refs[:share], refs[share : 2 * share]
    z, gain, out = refs[2 * share :]
    me = lax.rem(lax.axis_index("ctx"), share)
    chunk = firsts[0].shape[1]
    piece = 2 * chunk
    for m in range(share):
        base = pl.multiple_of((me ^ m) * piece, LANES)
        gated = []
        for c, source in enumerate((firsts[m], seconds[m])):
            gate = z[:, pl.ds(pl.multiple_of(base + c * chunk, LANES), chunk)].astype(f32)
            gated.append(source[...].astype(f32) * (gate * jax.nn.sigmoid(gate)))
        square = sum(jnp.sum(v * v, axis=1, keepdims=True) for v in gated)
        factor = lax.rsqrt(square / piece + norm_eps)
        for c, value in enumerate(gated):
            at = pl.ds(pl.multiple_of(base + c * chunk, LANES), chunk)
            out[:, at] = (value * factor * gain[:, at]).astype(bf16)


def attention_body(reach, q_ref, *refs):
    pieces, out = refs[: reach + 1], refs[reach + 1]
    rows = q_ref.shape[0]
    keys = rows * (reach + 1)
    padded = -(-keys // LANES) * LANES
    ratio = AH // KVH
    heads_wide = KVH * HD
    id_row = sum(p[rows : rows + 16, :].astype(f32)[15:16, :] for p in pieces)[:, :padded]
    own = pieces[0][rows : rows + 16, :].astype(f32)[15:16, :rows]
    square = iota((rows, rows), 0) == iota((rows, rows), 1)
    column = jnp.sum(
        jnp.where(square, jnp.broadcast_to(own, (rows, rows)), 0.0), axis=1, keepdims=True
    )
    lane = iota((rows, padded), 1)
    allowed = (id_row == column) & ((lane >= rows) | (lane <= iota((rows, padded), 0)))
    bias = jnp.where(allowed, 0.0, -1e30)
    pairs = ratio // 2
    bias = jnp.concatenate([bias] * pairs, axis=0)
    filler = [jnp.zeros((padded - keys, LANES), bf16)] if padded > keys else []
    even = iota((padded, LANES), 1) < HD
    nothing = jnp.zeros((padded, LANES), bf16)
    even_out = iota((rows * pairs, LANES), 1) < HD

    def both(at, side):
        whole = jnp.concatenate(
            [p[:rows, at : at + LANES] for p in pieces] + filler, axis=0
        ).astype(f32)
        kept = jnp.where(even == (side == 0), whole, 0.0)
        other = pltpu.roll(kept, HD, 1)
        first, second = (kept, other) if side == 0 else (other, kept)
        return jnp.concatenate([first.astype(bf16), second.astype(bf16)], axis=0)

    for g in range(KVH):
        block = (g // 2) * LANES
        key_pair = both(block, g % 2)
        value_pair = both(heads_wide + block, g % 2)
        base = g * ratio * HD
        q = jnp.concatenate(
            [q_ref[:, base + i * LANES : base + (i + 1) * LANES] for i in range(pairs)], axis=0
        )
        scores = lax.dot_general(
            q, key_pair, (((1,), (1,)), ((), ())), preferred_element_type=f32
        ) * (1.0 / math.sqrt(HD))
        probs, totals = [], []
        for side in range(2):
            masked = scores[:, side * padded : (side + 1) * padded] + bias
            top = jnp.max(masked, axis=1, keepdims=True)
            weight = jnp.exp(masked - top)
            totals.append(jnp.sum(weight, axis=1, keepdims=True))
            probs.append(weight.astype(bf16))
        mixed = jnp.dot(
            jnp.concatenate(probs, axis=1), value_pair, preferred_element_type=f32
        ) / jnp.where(even_out, totals[0], totals[1])
        for i in range(pairs):
            out[:, base + i * LANES : base + (i + 1) * LANES] = mixed[
                i * rows : (i + 1) * rows, :
            ].astype(bf16)


def gathered_attention(query, keys, values, own_ids):
    tokens_here = query.shape[0]
    place = lax.axis_index("ctx")
    all_ids = lax.all_gather(own_ids, "ctx", axis=0, tiled=True)
    ratio = AH // KVH
    queries = query.reshape(tokens_here, KVH, ratio, HD)
    query_pos = place * tokens_here + jnp.arange(tokens_here)
    key_piece = lax.all_gather(keys, "ctx", axis=0, tiled=True)
    value_piece = lax.all_gather(values, "ctx", axis=0, tiled=True)
    count = key_piece.shape[0]
    width = math.gcd(count, 512)
    key_blocks = key_piece.reshape(count // width, width, KVH, HD)
    value_blocks = value_piece.reshape(count // width, width, KVH, HD)
    shape = (KVH, ratio, tokens_here)

    def visit(running, item):
        key_block, value_block, order = item
        first = order * width
        key_ids = lax.dynamic_slice_in_dim(all_ids, first, width)
        key_pos = first + jnp.arange(width)
        allowed = (query_pos[:, None] >= key_pos[None, :]) & (own_ids[:, None] == key_ids[None, :])
        largest, totals, accum = running
        logits = jnp.einsum(
            "tgrd,mgd->grtm", queries, key_block, preferred_element_type=f32
        ) / math.sqrt(HD)
        masked = jnp.where(allowed, logits, -1e30)
        newest = jnp.maximum(largest, jnp.max(masked, axis=-1))
        weight = jnp.where(allowed, jnp.exp(masked - newest[..., None]), 0.0)
        correct = jnp.exp(largest - newest)
        totals = totals * correct + jnp.sum(weight, axis=-1)
        accum = accum * correct[..., None] + jnp.einsum(
            "grtm,mgd->grtd", weight.astype(bf16), value_block, preferred_element_type=f32
        )
        return (newest, totals, accum), None

    start = (jnp.full(shape, -1e30, f32), jnp.zeros(shape, f32), jnp.zeros(shape + (HD,), f32))
    (_, totals, accum), _ = lax.scan(
        visit, start, (key_blocks, value_blocks, jnp.arange(count // width, dtype=jnp.int32))
    )
    attended = accum / totals[..., None]
    return jnp.transpose(attended, (2, 0, 1, 3)).reshape(tokens_here, AH * HD).astype(bf16)


def on_device(
    x_in,
    z_in,
    bc_in,
    dt_raw,
    a_log,
    dt_bias,
    d_skip,
    conv_x,
    conv_bc,
    norm_gain,
    seg_ids,
    query,
    keys,
    values,
):
    ranks = lax.axis_size("ctx")
    rows, width = x_in.shape[1:]
    share = BLK // rows
    blocks = ranks // share
    piece = width // share
    chunk = piece // CHUNKS
    reach = -(-(rows * ranks // 2 - 1) // rows)
    shape = jax.ShapeDtypeStruct
    state_type = bf16 if blocks <= 2 else f32

    packed = call(
        functools.partial(pack_body, share, chunk),
        [shape((rows, chunk + 4 * LANES), bf16)] * share
        + [shape((rows, chunk), bf16)] * share
        + [shape((rows + 16, 4 * LANES), bf16)] * (share + 1),
        bytes_accessed=5 * 2**20,
    )(x_in[0], bc_in[0], dt_raw[0], seg_ids, keys[0], values[0])
    a_send, b_send, kv_send = packed[:share], packed[share : 2 * share], packed[2 * share :]
    order = [2, 3, 1]
    a_here, b_here = {0: a_send[0]}, {0: b_send[0]}
    for m in order:
        a_here[m] = crossed(a_send[m], "ctx", m)
    kv_here = [kv_send[0]] + [shifted(kv_send[r], "ctx", r) for r in range(1, share + 1)]
    for m in order:
        b_here[m] = crossed(b_send[m], "ctx", m)
    a_all = [a_here[m] for m in range(share)]
    b_all = [b_here[m] for m in range(share)]

    per_token = shape((BLK, LANES), f32)
    xc_a, bcc, state_a, ids_col, cum, step, writes, keep = call(
        functools.partial(first_body, share),
        [
            shape((BLK, chunk), bf16),
            shape((BLK, 2 * LANES), bf16),
            shape((LANES, chunk), state_type),
            shape((BLK + 8, LANES), f32),
            per_token,
            per_token,
            shape((BLK, LANES), bf16),
            per_token,
        ],
        scratch=[
            pltpu.VMEM((BLK + 8, chunk), f32),
            pltpu.VMEM((BLK + 8, 4 * LANES), f32),
            pltpu.VMEM((3, BLK, LANES), f32),
        ],
        flops=2**28,
        bytes_accessed=3 * 2**20,
    )(*kv_here[1:], *a_all, conv_x[0], conv_bc[0], dt_bias, a_log)
    xc_b, state_b = call(
        functools.partial(second_body, share),
        [shape((BLK, chunk), bf16), shape((LANES, chunk), state_type)],
        scratch=[pltpu.VMEM((BLK + 8, chunk), f32), pltpu.VMEM((3, BLK, LANES), f32)],
        flops=2**28,
        bytes_accessed=3 * 2**20,
    )(*kv_here[1:], *b_all, conv_x[0], bcc, ids_col, writes)

    def entering(state, first):
        if blocks > 2:
            heads = chunk // HD
            fade = jnp.repeat(keep[BLK - 1, first : first + heads], HD)[None, :]
            far = 1
            while far < blocks:
                came, came_fade = (
                    shifted(state, "ctx", far * share),
                    shifted(fade, "ctx", far * share),
                )
                state = state + fade * came
                fade = fade * came_fade
                far *= 2
        return shifted(state, "ctx", share).astype(bf16)

    entry_a = entering(state_a, 0)
    entry_b = entering(state_b, chunk // HD)

    local_a, local_b = call(
        functools.partial(mixing_body, share),
        [shape((BLK, chunk), f32)] * CHUNKS,
        flops=2**31,
        bytes_accessed=4 * 2**20,
    )(xc_a, xc_b, bcc, ids_col, cum, step, d_skip)

    if reach <= share:
        attended = call(
            functools.partial(attention_body, reach),
            shape((rows, AH * HD), bf16),
            flops=2**30,
            bytes_accessed=2**20,
        )(query[0], *kv_here[: reach + 1])
    else:
        attended = gathered_attention(query[0], keys[0], values[0], seg_ids[0])
    handoff = from_behind(attended, "pipe", 1)

    sent = []
    for c, (entry, local) in enumerate(((entry_a, local_a), (entry_b, local_b))):
        y = call(
            functools.partial(finish_kernel, share, c * (chunk // HD)),
            [shape((rows, chunk), bf16)] * share,
            scratch=[pltpu.VMEM((BLK, chunk), f32)],
            flops=2**28,
            bytes_accessed=2 * 2**20,
        )(entry, bcc, keep, local)
        here = {0: y[0]}
        for m in order:
            here[m] = crossed(y[m], "ctx", m)
        sent += [here[m] for m in range(share)]
    mamba_out = call(
        functools.partial(norm_body, share),
        shape((rows, width), bf16),
        bytes_accessed=3 * 2**20,
    )(*sent, z_in[0], norm_gain)
    return (mamba_out[None], handoff[None])


def solution(mesh):
    in_specs = (
        P("pipe", "ctx", None),
        P("pipe", "ctx", None),
        P("pipe", "ctx", None),
        P("pipe", "ctx", None),
        P("pipe", None),
        P("pipe", None),
        P("pipe", None),
        P("pipe", None, None),
        P("pipe", None, None),
        P("pipe", None),
        P("pipe", "ctx"),
        P("pipe", "ctx", None),
        P("pipe", "ctx", None),
        P("pipe", "ctx", None),
    )
    out_specs = (P("pipe", "ctx", None), P("pipe", "ctx", None))
    return jax.shard_map(
        on_device, mesh=mesh, in_specs=in_specs, out_specs=out_specs, check_vma=False
    )
```

```python
import functools
import math

import jax
import jax.numpy as jnp
from jax import lax
from jax.experimental import pallas as pl
from jax.experimental.pallas import tpu as pltpu
from jax.sharding import PartitionSpec as P

G = 4
AH = 32
KVH = 4
HD = 64
BLK = 256
LANES = 128
LOCAL_HEADS = 32
CHUNKS = 2
PACK_ROOM = 58
WHOLE = (False, False)

norm_eps = 1e-05
bf16 = jnp.bfloat16
f32 = jnp.float32


def shifted(value, axis, steps):
    count = lax.axis_size(axis)
    return lax.ppermute(value, axis, [(i, i + steps) for i in range(count - steps)])


def turned_on(value, axis, steps):
    count = lax.axis_size(axis)
    return lax.ppermute(value, axis, [(i, (i + steps) % count) for i in range(count)])


def crossed(value, axis, mask):
    count = lax.axis_size(axis)
    return lax.ppermute(value, axis, [(i, i ^ mask) for i in range(count)])


def iota(shape, dim):
    return lax.broadcasted_iota(jnp.int32, shape, dim)


def call(body, outs, scratch=(), flops=0, bytes_accessed=0, room=48, **specs):
    return pl.pallas_call(
        body,
        out_shape=outs,
        scratch_shapes=list(scratch),
        compiler_params=pltpu.CompilerParams(vmem_limit_bytes=int(room * 2**20)),
        cost_estimate=pl.CostEstimate(
            flops=flops, bytes_accessed=bytes_accessed, transcendentals=0
        ),
        **specs,
    )


def hbm():
    return pl.BlockSpec(memory_space=pltpu.HBM)


def vmem():
    return pl.BlockSpec(memory_space=pltpu.VMEM)


def pack_body(share, x_hbm, bc_hbm, dt_hbm, ids_ref, k_hbm, v_hbm, *refs):
    sends, seconds = refs[:share], refs[share : 2 * share]
    own_kv, near_kv, far_kv, bc_ref, dt_ref, sems, tails = refs[2 * share :]
    me = lax.rem(lax.axis_index("ctx"), share)
    rows, width = x_hbm.shape
    piece = width // share
    chunk = piece // CHUNKS
    states = bc_hbm.shape[1] // (2 * G)
    wide = 4 * LANES
    copies = [
        pltpu.make_async_copy(bc_hbm, bc_ref, sems.at[0]),
        pltpu.make_async_copy(dt_hbm, dt_ref, sems.at[1]),
    ]
    for m in (2, 3, 1, 0):
        for c, target in enumerate((sends[m].at[:, pl.ds(0, chunk)], seconds[m])):
            base = pl.multiple_of((me ^ m) * piece + c * chunk, LANES)
            copies.append(
                pltpu.make_async_copy(
                    x_hbm.at[:, pl.ds(base, chunk)], target, sems.at[2 + share * c + m]
                )
            )
    for i, kv in enumerate((own_kv, near_kv, far_kv)):
        for side, source in enumerate((k_hbm, v_hbm)):
            copies.append(
                pltpu.make_async_copy(
                    source,
                    kv.at[pl.ds(0, rows), pl.ds(side * wide // 2, wide // 2)],
                    sems.at[2 + 2 * share + 2 * i + side],
                )
            )
    copies.append(
        pltpu.make_async_copy(x_hbm.at[pl.ds(rows - 16, 16), :], tails, sems.at[2 * share + 8])
    )
    for copy in copies:
        copy.start()
    number = ids_ref[...].astype(f32) + 1.0
    square = iota((rows, rows), 0) == iota((rows, rows), 1)
    column = jnp.sum(
        jnp.where(square, jnp.broadcast_to(number, (rows, rows)), 0.0), axis=1, keepdims=True
    )
    lane = iota((rows, wide), 1)
    row = iota((rows, wide), 0)
    which = iota((16, wide), 0)
    small = iota((rows, LANES), 1)
    copies[0].wait()
    copies[1].wait()
    steps = dt_ref[...].astype(f32)

    def head_part(s):
        turned = pltpu.roll(steps, lax.rem(LANES - LOCAL_HEADS * s, LANES), 1)
        return jnp.where(small < LOCAL_HEADS, turned, column)

    for m in (2, 3, 1, 0):
        s = me ^ m
        b_at = pl.multiple_of(s * states, LANES)
        c_at = pl.multiple_of(G * states + s * states, LANES)
        sends[m][:, chunk : chunk + states] = bc_ref[:, pl.ds(b_at, states)]
        sends[m][:, chunk + states : chunk + 2 * states] = bc_ref[:, pl.ds(c_at, states)]
        sends[m][:, chunk + 2 * states :] = head_part(s).astype(bf16)
    for copy in copies[2:]:
        copy.wait()
    last = slice(rows - 16, rows)
    for slot, kv in enumerate((own_kv, near_kv, far_kv)):
        at = jnp.where(lane >= 3 * rows, lane - 3 * rows, lane)
        id_row = jnp.sum(jnp.where(at == row + rows * slot, column, 0.0), axis=0, keepdims=True)
        if slot == 0:
            kv[rows:, :] = jnp.where(which == 15, id_row, 0.0).astype(bf16)
            continue
        for part in range(2):
            s = 2 * (slot - 1) + part
            block = jnp.where(which == 15, id_row, 0.0)
            blocks = [
                tails[:, s * piece + p * wide : s * piece + (p + 1) * wide].astype(f32)
                for p in range(piece // wide)
            ]
            blocks.append(
                jnp.concatenate(
                    [
                        bc_ref[last, s * states : (s + 1) * states].astype(f32),
                        bc_ref[last, (G + s) * states : (G + s + 1) * states].astype(f32),
                        jnp.broadcast_to(column[last, :], (16, 2 * LANES)),
                    ],
                    axis=1,
                )
            )
            for i in range(3):
                for p, source in enumerate(blocks):
                    block = jnp.where(which == 5 * i + p, source[13 + i : 14 + i, :], block)
            kv[rows + 16 * part : rows + 16 * (part + 1), :] = block.astype(bf16)


def pick_halo(me, rows, mine, other):
    count = rows + 16
    second = count + rows
    third = second + rows + 32
    options = [
        other[second : second + 16, :],
        mine[second + 16 : second + 32, :],
        other[third : third + 16, :],
        mine[third + 16 : third + 32, :],
    ]
    picked = options[0].astype(f32)
    for j in range(1, 4):
        picked = jnp.where(me == j, options[j].astype(f32), picked)
    return jnp.where(lax.axis_index("ctx") >= 4, picked, 0.0)


def place_halo(scratch, picked, pieces):
    wide = picked.shape[1]
    for at, p in enumerate(pieces):
        which = iota((8, wide), 0)
        block = jnp.zeros((8, wide), f32)
        for i in range(3):
            block = jnp.where(which == 5 + i, picked[5 * i + p : 5 * i + p + 1, :], block)
        scratch[0:8, at * wide : (at + 1) * wide] = block


def conv_strip(src, columns, masks, taps):
    length = masks.shape[1]
    total = None
    for tap in range(4):
        term = taps[tap] * src[5 + tap : 5 + tap + length, columns]
        if tap < 3:
            term = term * masks[tap]
        total = term if total is None else total + term
    return (total * jax.nn.sigmoid(total)).astype(bf16)


def set_masks(masks, ids):
    length = masks.shape[1]
    own = ids[8 : 8 + length, :]
    for tap in range(3):
        masks[tap] = jnp.where(ids[5 + tap : 5 + tap + length, :] == own, 1.0, 0.0)


def taps_at(conv_ref, at):
    weights = conv_ref[:, pl.ds(pl.multiple_of(at, LANES), LANES)].astype(f32)
    return [weights[t : t + 1, :] for t in range(4)]


def one_hot(first, chunk):
    lane = iota((LANES, chunk), 0)
    head = iota((LANES, chunk), 1) // HD + first
    return jnp.where((lane % LOCAL_HEADS == head) & (lane < 3 * LOCAL_HEADS), 1.0, 0.0).astype(bf16)


def three_parts(value):
    lane = iota(value.shape, 1)
    high = value.astype(bf16).astype(f32)
    rest = value - high
    middle = rest.astype(bf16).astype(f32)
    low = rest - middle
    packed = jnp.where(
        lane < LOCAL_HEADS,
        high,
        jnp.where(
            lane < 2 * LOCAL_HEADS,
            pltpu.roll(middle, LOCAL_HEADS, 1),
            jnp.where(lane < 3 * LOCAL_HEADS, pltpu.roll(low, 2 * LOCAL_HEADS, 1), 0.0),
        ),
    )
    return packed.astype(bf16)


def conv_x_and_state(xs, masks, conv_ref, base, bcc, writes, first, xc_ref, state_ref):
    chunk = xc_ref.shape[1]
    for c in range(chunk // LANES):
        columns = slice(c * LANES, (c + 1) * LANES)
        xc_ref[:, columns] = conv_strip(xs, columns, masks, taps_at(conv_ref, base + c * LANES))
    factors = jnp.dot(writes, one_hot(first, chunk), preferred_element_type=f32)
    scaled = (xc_ref[...].astype(f32) * factors).astype(bf16)
    state = lax.dot_general(bcc, scaled, (((0,), (0,)), ((), ())), preferred_element_type=f32)
    state_ref[...] = state.astype(state_ref.dtype)


def turned(row, me):
    return pltpu.roll(
        jnp.broadcast_to(row, (8, LANES)), lax.rem(LANES - LOCAL_HEADS * me, LANES), 1
    )


def first_body(share, with_halo, *refs):
    pieces = refs[:share]
    convx, convbc, bias, alog = refs[share : share + 4]
    rest = refs[share + 4 :]
    me = lax.rem(lax.axis_index("ctx"), share)
    if with_halo:
        picked = pick_halo(me, pieces[0].shape[0], rest[0], rest[1])
        rest = rest[2:]
    xc_o, bcc_o, state_o, ids_o, cum_o, step_o, writes_o, xs, bs, masks = rest
    chunk = xc_o.shape[1]
    piece = chunk * CHUNKS
    rows = pieces[0].shape[0]
    length = rows * share
    per_block = 4 * LANES
    if with_halo:
        place_halo(xs, picked, list(range(chunk // per_block)))
        place_halo(bs, picked, [4])
    else:
        xs[0:8, :] = jnp.zeros((8, chunk), f32)
        bs[0:8, :] = jnp.zeros((8, per_block), f32)
    for m in range(share):
        at = pl.multiple_of(8 + rows * (me ^ m), 8)
        xs[pl.ds(at, rows), :] = pieces[m][:, :chunk].astype(f32)
        bs[pl.ds(at, rows), : 3 * LANES] = pieces[m][:, chunk:].astype(f32)
    where_ids = 2 * LANES + LOCAL_HEADS
    ids_o[...] = jnp.broadcast_to(bs[:, where_ids : where_ids + 1], (length + 8, LANES))
    set_masks(masks, ids_o)
    for half in range(2):
        columns = slice(half * LANES, (half + 1) * LANES)
        taps = taps_at(convbc, half * G * LANES + me * LANES)
        bcc_o[:, columns] = conv_strip(bs, columns, masks, taps)
    raw = bs[8:, 2 * LANES : 3 * LANES] + turned(bias[...], me)[0:1, :]
    step = jnp.maximum(raw, 0.0) + jnp.log1p(jnp.exp(-jnp.abs(raw)))
    total = step * (-jnp.exp(turned(alog[...], me)[0:1, :]))
    row = iota((length, LANES), 0)
    reach = 1
    while reach < length:
        total = total + jnp.where(row >= reach, pltpu.roll(total, reach, 0), 0.0)
        reach *= 2
    own = ids_o[8:, :]
    last = length - 1
    writes = (
        jnp.where(own == own[last : last + 1, :], jnp.exp(total[last : last + 1, :] - total), 0.0)
        * step
    )
    cum_o[...] = total
    step_o[...] = step
    packed = three_parts(writes)
    writes_o[...] = packed
    conv_x_and_state(xs, masks, convx, me * piece, bcc_o[:, :LANES], packed, 0, xc_o, state_o)


def second_body(share, with_halo, *refs):
    pieces = refs[:share]
    convx, bcc, ids, writes = refs[share : share + 4]
    rest = refs[share + 4 :]
    me = lax.rem(lax.axis_index("ctx"), share)
    if with_halo:
        picked = pick_halo(me, pieces[0].shape[0], rest[0], rest[1])
        rest = rest[2:]
    xc_o, state_o, xs, masks = rest
    chunk = xc_o.shape[1]
    rows = pieces[0].shape[0]
    blocks = chunk // (4 * LANES)
    if with_halo:
        place_halo(xs, picked, list(range(blocks, 2 * blocks)))
    else:
        xs[0:8, :] = jnp.zeros((8, chunk), f32)
    for m in range(share):
        at = pl.multiple_of(8 + rows * (me ^ m), 8)
        xs[pl.ds(at, rows), :] = pieces[m][...].astype(f32)
    set_masks(masks, ids)
    base = me * (chunk * CHUNKS) + chunk
    conv_x_and_state(
        xs, masks, convx, base, bcc[:, :LANES], writes[...], chunk // HD, xc_o, state_o
    )


def mixing_body(share, *refs):
    pieces, seconds = refs[:share], refs[share : 2 * share]
    xcs, refs = refs[2 * share : 2 * share + CHUNKS], refs[2 * share + CHUNKS :]
    mine, other, convx, convbc, bcc_in, cum, step, skip = refs[:8]
    rest = refs[8:]
    outs, (bcc, keep, head, head_ids, masks, first_x) = rest[:CHUNKS], rest[CHUNKS:]
    me = lax.rem(lax.axis_index("ctx"), share)
    length, chunk = xcs[0].shape
    rows = pieces[0].shape[0]
    piece = chunk * CHUNKS
    half = length // 2
    picked = pick_halo(me, rows, mine, other)
    place_halo(head, picked, list(range(5)))

    def first_rows(buffers, columns):
        start = buffers[0][:16, columns].astype(f32)
        for m in range(1, share):
            start = jnp.where(me == m, buffers[m][:16, columns].astype(f32), start)
        return start

    head[8:, :chunk] = first_rows(pieces, slice(0, chunk))
    head[8:, chunk:piece] = first_rows(seconds, slice(0, chunk))
    head[8:, piece : piece + 3 * LANES] = first_rows(pieces, slice(chunk, chunk + 3 * LANES))
    where_ids = piece + 2 * LANES + LOCAL_HEADS
    head_ids[...] = jnp.broadcast_to(head[:, where_ids : where_ids + 1], (24, LANES))
    set_masks(masks, head_ids)
    for c in range(piece // LANES):
        columns = slice(c * LANES, (c + 1) * LANES)
        first_x[:, columns] = conv_strip(
            head, columns, masks, taps_at(convx, me * piece + c * LANES)
        )
    bcc[16:, :] = bcc_in[16:, :]
    for side in range(2):
        columns = slice(piece + side * LANES, piece + (side + 1) * LANES)
        taps = taps_at(convbc, side * G * LANES + me * LANES)
        bcc[:16, side * LANES : (side + 1) * LANES] = conv_strip(head, columns, masks, taps)

    inner = lax.dot_general(
        bcc[:, LANES:], bcc[:, :LANES], (((1,), (1,)), ((), ())), preferred_element_type=f32
    )
    ids = []
    for i in range(share):
        part = pieces[0][:, chunk + 2 * LANES :].astype(f32)
        for m in range(1, share):
            part = jnp.where((me ^ m) == i, pieces[m][:, chunk + 2 * LANES :].astype(f32), part)
        ids.append(part)
    ids = jnp.concatenate(ids, axis=0)
    across = ids.T[LOCAL_HEADS : LOCAL_HEADS + 1, :]
    own = jnp.broadcast_to(ids[:, LOCAL_HEADS : LOCAL_HEADS + 1], (length, length))
    allowed = (iota((length, length), 0) >= iota((length, length), 1)) & (own == across)
    inner = jnp.where(allowed, inner, 0.0)
    cums = cum[...]
    keep[...] = jnp.where(own[:, :LANES] == head_ids[7:8, :], jnp.exp(cums), 0.0)
    cum_rows = cums.T
    step_rows = step[...].T
    gains = three_parts(turned(skip[...], me))
    even = iota((half, LANES), 1) < HD
    for c in range(CHUNKS):
        first = c * (chunk // HD)
        spread = jnp.dot(gains, one_hot(first, chunk), preferred_element_type=f32)[0:1, :]
        for pair in range(chunk // LANES):
            columns = slice(pair * LANES, (pair + 1) * LANES)
            x_pair = jnp.concatenate(
                [
                    first_x[:, c * chunk + pair * LANES : c * chunk + (pair + 1) * LANES],
                    xcs[c][16:, columns],
                ],
                axis=0,
            )
            upper, lower = [], []
            for side in range(2):
                h = first + 2 * pair + side
                fade = cum_rows[h : h + 1, :]
                size = step_rows[h : h + 1, :]
                col = cums[:, h : h + 1]
                top = (
                    inner[:half, :half]
                    * (jnp.exp(jnp.minimum(col[:half] - fade[:, :half], 0.0)) * size[:, :half])
                ).astype(bf16)
                low = (
                    inner[half:, :] * (jnp.exp(jnp.minimum(col[half:] - fade, 0.0)) * size)
                ).astype(bf16)
                upper.append(jnp.dot(top, x_pair[:half, :], preferred_element_type=f32))
                lower.append(jnp.dot(low, x_pair, preferred_element_type=f32))
            gain = spread[:, columns]
            outs[c][:half, columns] = jnp.where(even, upper[0], upper[1]) + gain * x_pair[
                :half, :
            ].astype(f32)
            outs[c][half:, columns] = jnp.where(even, lower[0], lower[1]) + gain * x_pair[
                half:, :
            ].astype(f32)


def finish_body(share, first, state, bcc, keep, local, *rest):
    outs, total = rest[:-1], rest[-1]
    me = lax.rem(lax.axis_index("ctx"), share)
    chunk = local.shape[1]
    rows = outs[0].shape[-2]
    carried = jnp.dot(bcc[:, LANES:], state[...], preferred_element_type=f32)
    factors = jnp.dot(three_parts(keep[...]), one_hot(first, chunk), preferred_element_type=f32)
    total[...] = local[...] + carried * factors
    if len(outs) == 1:
        for i in range(share):
            outs[0][i] = total[rows * i : rows * (i + 1), :].astype(bf16)
        return
    for m in range(share):
        at = pl.multiple_of(rows * (me ^ m), rows)
        outs[m][...] = total[pl.ds(at, rows), :].astype(bf16)


def norm_body(share, *refs):
    z, gain, handed, out, handoff, buffer, sems = refs[-7:]
    me = lax.rem(lax.axis_index("ctx"), share)
    chunk = refs[0].shape[-1]
    parts, at = [], 0
    for whole in WHOLE:
        if whole:
            parts.append([lambda m, r=refs[at]: r[me ^ m]])
            at += 1
        else:
            parts.append([lambda m, r=refs[at : at + share]: r[m][...]])
            at += share
    piece = 2 * chunk
    copies = [pltpu.make_async_copy(handed, handoff, sems.at[share])]
    copies[0].start()
    for m in (0, 2, 3, 1):
        base = pl.multiple_of((me ^ m) * piece, LANES)
        gated = []
        for c, (source,) in enumerate(parts):
            gate = z[:, pl.ds(pl.multiple_of(base + c * chunk, LANES), chunk)].astype(f32)
            gated.append(source(m).astype(f32) * (gate * jax.nn.sigmoid(gate)))
        square = sum(jnp.sum(v * v, axis=1, keepdims=True) for v in gated)
        factor = lax.rsqrt(square / piece + norm_eps)
        for c, value in enumerate(gated):
            at = pl.ds(pl.multiple_of(base + c * chunk, LANES), chunk)
            buffer[m, :, c * chunk : (c + 1) * chunk] = (value * factor * gain[:, at]).astype(bf16)
        copies.append(
            pltpu.make_async_copy(buffer.at[m], out.at[:, pl.ds(base, piece)], sems.at[m])
        )
        copies[-1].start()
    for copy in copies:
        copy.wait()


def attention_body(q_ref, mine, other, out):
    rows = q_ref.shape[0]
    keys = 6 * rows
    ratio = AH // KVH
    heads_wide = KVH * HD
    here = lax.axis_index("ctx")
    odd = lax.rem(here, 2) == 1
    starts = (0, rows + 16, 2 * rows + 48)

    def id_rows(buffer):
        total = None
        for at in starts:
            row = buffer[at + rows : at + rows + 16, :].astype(f32)[15:16, :keys]
            total = row if total is None else total + row
        return total

    lane_row = iota((1, keys), 1)
    id_row = jnp.where(lane_row < 3 * rows, id_rows(mine), id_rows(other))
    own = mine[rows : rows + 16, :].astype(f32)[15:16, :rows]
    square = iota((rows, rows), 0) == iota((rows, rows), 1)
    column = jnp.sum(
        jnp.where(square, jnp.broadcast_to(own, (rows, rows)), 0.0), axis=1, keepdims=True
    )
    lane = iota((rows, keys), 1)
    earlier = (lane >= rows) | (lane <= iota((rows, keys), 0))
    sibling = (lane < 3 * rows) | (lane >= 4 * rows) | odd
    slot = lane % (3 * rows) // rows
    before = (slot == 0) | ((slot == 1) & (here >= 2)) | ((slot == 2) & (here >= 4))
    bias = jnp.where((id_row == column) & earlier & sibling & before, 0.0, -1e30)
    pairs = ratio // 2
    bias = jnp.concatenate([bias] * pairs, axis=0)
    even = iota((keys, LANES), 1) < HD
    even_out = iota((rows * pairs, LANES), 1) < HD

    def both(at, side):
        whole = jnp.concatenate(
            [b[s : s + rows, at : at + LANES] for b in (mine, other) for s in starts], axis=0
        ).astype(f32)
        kept = jnp.where(even == (side == 0), whole, 0.0)
        moved = pltpu.roll(kept, HD, 1)
        first, second = (kept, moved) if side == 0 else (moved, kept)
        return jnp.concatenate([first.astype(bf16), second.astype(bf16)], axis=0)

    for g in range(KVH):
        block = (g // 2) * LANES
        key_pair = both(block, g % 2)
        value_pair = both(heads_wide + block, g % 2)
        base = g * ratio * HD
        q = jnp.concatenate(
            [q_ref[:, base + i * LANES : base + (i + 1) * LANES] for i in range(pairs)], axis=0
        )
        scores = lax.dot_general(
            q, key_pair, (((1,), (1,)), ((), ())), preferred_element_type=f32
        ) * (1.0 / math.sqrt(HD))
        probs, totals = [], []
        for side in range(2):
            masked = scores[:, side * keys : (side + 1) * keys] + bias
            top = jnp.max(masked, axis=1, keepdims=True)
            weight = jnp.exp(masked - top)
            totals.append(jnp.sum(weight, axis=1, keepdims=True))
            probs.append(weight.astype(bf16))
        mixed = jnp.dot(
            jnp.concatenate(probs, axis=1), value_pair, preferred_element_type=f32
        ) / jnp.where(even_out, totals[0], totals[1])
        for i in range(pairs):
            out[:, base + i * LANES : base + (i + 1) * LANES] = mixed[
                i * rows : (i + 1) * rows, :
            ].astype(bf16)


def gathered_attention(query, keys, values, own_ids):
    tokens_here = query.shape[0]
    place = lax.axis_index("ctx")
    all_ids = lax.all_gather(own_ids, "ctx", axis=0, tiled=True)
    ratio = AH // KVH
    queries = query.reshape(tokens_here, KVH, ratio, HD)
    query_pos = place * tokens_here + jnp.arange(tokens_here)
    key_piece = lax.all_gather(keys, "ctx", axis=0, tiled=True)
    value_piece = lax.all_gather(values, "ctx", axis=0, tiled=True)
    count = key_piece.shape[0]
    width = math.gcd(count, 512)
    key_blocks = key_piece.reshape(count // width, width, KVH, HD)
    value_blocks = value_piece.reshape(count // width, width, KVH, HD)
    shape = (KVH, ratio, tokens_here)

    def visit(running, item):
        key_block, value_block, order = item
        first = order * width
        key_ids = lax.dynamic_slice_in_dim(all_ids, first, width)
        key_pos = first + jnp.arange(width)
        allowed = (query_pos[:, None] >= key_pos[None, :]) & (own_ids[:, None] == key_ids[None, :])
        largest, totals, accum = running
        logits = jnp.einsum(
            "tgrd,mgd->grtm", queries, key_block, preferred_element_type=f32
        ) / math.sqrt(HD)
        masked = jnp.where(allowed, logits, -1e30)
        newest = jnp.maximum(largest, jnp.max(masked, axis=-1))
        weight = jnp.where(allowed, jnp.exp(masked - newest[..., None]), 0.0)
        correct = jnp.exp(largest - newest)
        totals = totals * correct + jnp.sum(weight, axis=-1)
        accum = accum * correct[..., None] + jnp.einsum(
            "grtm,mgd->grtd", weight.astype(bf16), value_block, preferred_element_type=f32
        )
        return (newest, totals, accum), None

    start = (jnp.full(shape, -1e30, f32), jnp.zeros(shape, f32), jnp.zeros(shape + (HD,), f32))
    (_, totals, accum), _ = lax.scan(
        visit, start, (key_blocks, value_blocks, jnp.arange(count // width, dtype=jnp.int32))
    )
    attended = accum / totals[..., None]
    return jnp.transpose(attended, (2, 0, 1, 3)).reshape(tokens_here, AH * HD).astype(bf16)


def on_device(
    x_in,
    z_in,
    bc_in,
    dt_raw,
    a_log,
    dt_bias,
    d_skip,
    conv_x,
    conv_bc,
    norm_gain,
    seg_ids,
    query,
    keys,
    values,
):
    ranks = lax.axis_size("ctx")
    rows, width = x_in.shape[1:]
    share = BLK // rows
    blocks = ranks // share
    piece = width // share
    chunk = piece // CHUNKS
    reach = -(-(rows * ranks // 2 - 1) // rows)
    shape = jax.ShapeDtypeStruct
    state_type = bf16 if blocks <= 2 else f32

    wide = 4 * LANES
    packed = call(
        functools.partial(pack_body, share),
        [shape((rows, chunk + 3 * LANES), bf16)] * share
        + [shape((rows, chunk), bf16)] * share
        + [shape((rows + 16, wide), bf16)]
        + [shape((rows + 32, wide), bf16)] * 2,
        scratch=[
            pltpu.VMEM((rows, bc_in.shape[2]), bf16),
            pltpu.VMEM((rows, LANES), bf16),
            pltpu.SemaphoreType.DMA((2 * share + 9,)),
            pltpu.VMEM((16, width), bf16),
        ],
        in_specs=[hbm()] * 3 + [vmem()] + [hbm()] * 2,
        room=PACK_ROOM,
        bytes_accessed=5 * 2**20,
    )(x_in[0], bc_in[0], dt_raw[0], seg_ids, keys[0], values[0])
    send, send_b, (kv_own, kv_near, kv_far) = (
        packed[:share],
        packed[share : 2 * share],
        packed[2 * share :],
    )
    order = [2, 3, 1]

    def exchanged(values):
        here = {0: values[0]}
        for m in order:
            here[m] = crossed(values[m], "ctx", m)
        return [here[m] for m in range(share)]

    pieces = exchanged(send)
    near, far = turned_on(kv_near, "ctx", 2), turned_on(kv_far, "ctx", 4)
    pieces_b = exchanged(send_b)
    halo = []
    if blocks > 2:
        mine = jnp.concatenate([kv_own, near, far], axis=0)
        other = crossed(mine, "ctx", 1)
        halo = [mine, other]
    per_token = shape((BLK, LANES), f32)
    xc_a, bcc_first, state_a, ids_col, cum, step, writes = call(
        functools.partial(first_body, share, blocks > 2),
        [
            shape((BLK, chunk), bf16),
            shape((BLK, 2 * LANES), bf16),
            shape((LANES, chunk), state_type),
            shape((BLK + 8, LANES), f32),
            per_token,
            per_token,
            shape((BLK, LANES), bf16),
        ],
        scratch=[
            pltpu.VMEM((BLK + 8, chunk), f32),
            pltpu.VMEM((BLK + 8, wide), f32),
            pltpu.VMEM((3, BLK, LANES), f32),
        ],
        flops=2**28,
        bytes_accessed=3 * 2**20,
    )(*pieces, conv_x[0], conv_bc[0], dt_bias, a_log, *halo)
    if blocks <= 2:
        near, far, cum = lax.optimization_barrier((near, far, cum))
        mine = jnp.concatenate([kv_own, near, far], axis=0)
        other = crossed(mine, "ctx", 1)
    xc_b, state_b = call(
        functools.partial(second_body, share, blocks > 2),
        [shape((BLK, chunk), bf16), shape((LANES, chunk), state_type)],
        scratch=[pltpu.VMEM((BLK + 8, chunk), f32), pltpu.VMEM((3, BLK, LANES), f32)],
        flops=2**28,
        bytes_accessed=3 * 2**20,
    )(*pieces_b, conv_x[0], bcc_first, ids_col, writes, *halo)
    per_head = chunk // HD

    def entering(state, first):
        if blocks > 2:
            same = ids_col[BLK + 7, :] == ids_col[7, :]
            fade = jnp.where(same, jnp.exp(cum[BLK - 1, :]), 0.0)[first : first + per_head]
            fade = jnp.repeat(fade, HD)[None, :]
            far = 1
            while far < blocks:
                came = shifted(state, "ctx", far * share)
                came_fade = shifted(fade, "ctx", far * share)
                state = state + fade * came
                fade = fade * came_fade
                far *= 2
        return turned_on(state, "ctx", share).astype(bf16)

    entry_a = entering(state_a, 0)
    entry_b = entering(state_b, per_head)

    local_a, local_b, bcc, keep = call(
        functools.partial(mixing_body, share),
        [shape((BLK, chunk), f32)] * CHUNKS + [shape((BLK, 2 * LANES), bf16), per_token],
        scratch=[
            pltpu.VMEM((24, piece + wide), f32),
            pltpu.VMEM((24, LANES), f32),
            pltpu.VMEM((3, 16, LANES), f32),
            pltpu.VMEM((16, piece), bf16),
        ],
        flops=2**31,
        bytes_accessed=4 * 2**20,
    )(*pieces, *pieces_b, xc_a, xc_b, mine, other, conv_x[0], conv_bc[0], bcc_first, cum, step, d_skip)

    if reach <= share:
        attended = call(
            attention_body,
            shape((rows, AH * HD), bf16),
            flops=2**30,
            bytes_accessed=2**20,
        )(query[0], mine, other)
    else:
        attended = gathered_attention(query[0], keys[0], values[0], seg_ids[0])
    local_a, attended = lax.optimization_barrier((local_a, attended))
    handoff = turned_on(attended, "pipe", 1)

    sent = []
    for c, (entry, local) in enumerate(((entry_a, local_a), (entry_b, local_b))):
        y = call(
            functools.partial(finish_body, share, c * per_head),
            [shape((share, rows, chunk), bf16)] if WHOLE[c] else [shape((rows, chunk), bf16)] * share,
            scratch=[pltpu.VMEM((BLK, chunk), f32)],
            flops=2**28,
            bytes_accessed=2 * 2**20,
        )(entry, bcc, keep, local)
        if WHOLE[c]:
            groups = [[b * share + i for i in range(share)] for b in range(blocks)]
            sent.append(
                lax.all_to_all(y[0], "ctx", 0, 0, tiled=True, axis_index_groups=groups)
            )
            continue
        sent += exchanged(y)
    mamba_out, handoff = call(
        functools.partial(norm_body, share),
        [shape((rows, width), bf16), shape((rows, AH * HD), bf16)],
        scratch=[pltpu.VMEM((share, rows, piece), bf16), pltpu.SemaphoreType.DMA((share + 1,))],
        out_specs=[hbm()] * 2,
        bytes_accessed=3 * 2**20,
    )(*sent, z_in[0], norm_gain, handoff)
    return (mamba_out[None], handoff[None])


def solution(mesh):
    in_specs = (
        P("pipe", "ctx", None),
        P("pipe", "ctx", None),
        P("pipe", "ctx", None),
        P("pipe", "ctx", None),
        P("pipe", None),
        P("pipe", None),
        P("pipe", None),
        P("pipe", None, None),
        P("pipe", None, None),
        P("pipe", None),
        P("pipe", "ctx"),
        P("pipe", "ctx", None),
        P("pipe", "ctx", None),
        P("pipe", "ctx", None),
    )
    out_specs = (P("pipe", "ctx", None), P("pipe", "ctx", None))
    return jax.shard_map(
        on_device, mesh=mesh, in_specs=in_specs, out_specs=out_specs, check_vma=False
    )
```

```python
import functools
import math

import jax
import jax.numpy as jnp
from jax import lax
from jax.experimental import pallas as pl
from jax.experimental.pallas import tpu as pltpu
from jax.sharding import PartitionSpec as P

G = 4
AH = 32
KVH = 4
HD = 64
BLK = 256
LANES = 128
LOCAL_HEADS = 32
CHUNKS = 2
PACK_ROOM = 58
WHOLE = (False, False)

norm_eps = 1e-05
bf16 = jnp.bfloat16
f32 = jnp.float32


def shifted(value, axis, steps):
    count = lax.axis_size(axis)
    return lax.ppermute(value, axis, [(i, i + steps) for i in range(count - steps)])


def turned_on(value, axis, steps):
    count = lax.axis_size(axis)
    return lax.ppermute(value, axis, [(i, (i + steps) % count) for i in range(count)])


def crossed(value, axis, mask):
    count = lax.axis_size(axis)
    return lax.ppermute(value, axis, [(i, i ^ mask) for i in range(count)])


def iota(shape, dim):
    return lax.broadcasted_iota(jnp.int32, shape, dim)


def call(body, outs, scratch=(), flops=0, bytes_accessed=0, room=48, **specs):
    return pl.pallas_call(
        body,
        out_shape=outs,
        scratch_shapes=list(scratch),
        compiler_params=pltpu.CompilerParams(vmem_limit_bytes=int(room * 2**20)),
        cost_estimate=pl.CostEstimate(
            flops=flops, bytes_accessed=bytes_accessed, transcendentals=0
        ),
        **specs,
    )


def hbm():
    return pl.BlockSpec(memory_space=pltpu.HBM)


def vmem():
    return pl.BlockSpec(memory_space=pltpu.VMEM)


def pack_body(share, x_hbm, bc_hbm, dt_hbm, ids_ref, k_hbm, v_hbm, *refs):
    sends, seconds = refs[:share], refs[share]
    kvs, rest = refs[share + 1 : share + 4], refs[share + 4 :]
    dt_ref, bc_ref, x_firsts, x_seconds, kv_ref, marks, own_extra, near_extra, far_extra = rest[:-2]
    x_tail, sems = rest[-2:]
    extras = (own_extra, near_extra, far_extra)
    me = lax.rem(lax.axis_index("ctx"), share)
    rows, width = x_hbm.shape
    piece = width // share
    chunk = piece // CHUNKS
    states = bc_hbm.shape[1] // (2 * G)
    wide = 4 * LANES
    started = []

    def start(source, target):
        copy = pltpu.make_async_copy(source, target, sems.at[len(started)])
        copy.start()
        started.append(copy)
        return copy

    order = (2, 3, 1, 0)
    steps_in, small_in = start(dt_hbm, dt_ref), start(bc_hbm, bc_ref)
    parts_in = []
    for c, held in enumerate((x_firsts, x_seconds)):
        for m in order:
            at = pl.multiple_of((me ^ m) * piece + c * chunk, LANES)
            if c == 0:
                parts_in.append(start(x_hbm.at[:, pl.ds(at, chunk)], held.at[m]))
            else:
                at = m * piece + chunk
                parts_in.append(start(x_hbm.at[:, pl.ds(at, chunk)], held.at[m]))
    kv_in = [
        start(source, kv_ref.at[:, pl.ds(side * wide // 2, wide // 2)])
        for side, source in enumerate((k_hbm, v_hbm))
    ]
    tail_in = start(x_hbm.at[pl.ds(rows - 16, 16), :], x_tail)
    arriving = len(started)
    number = ids_ref[...].astype(f32) + 1.0
    square = iota((rows, rows), 0) == iota((rows, rows), 1)
    column = jnp.sum(
        jnp.where(square, jnp.broadcast_to(number, (rows, rows)), 0.0), axis=1, keepdims=True
    )
    small = iota((rows, LANES), 1)
    steps_in.wait()
    steps = dt_ref[...].astype(f32)
    small_in.wait()
    for m in order:
        s = me ^ m
        turn = lax.rem(LANES - LOCAL_HEADS * s, LANES)
        marked = jnp.where(small < LOCAL_HEADS, pltpu.roll(steps, turn, 1), column).astype(bf16)
        for side in range(2):
            at = pl.multiple_of((side * G + s) * states, LANES)
            marks[m, :, side * states : (side + 1) * states] = bc_ref[:, pl.ds(at, states)]
        marks[m, :, 2 * states :] = marked
        start(marks.at[m], sends[m].at[:, pl.ds(chunk, 2 * states + LANES)])
    for i, m in enumerate(order):
        parts_in[i].wait()
        start(x_firsts.at[m], sends[m].at[:, pl.ds(0, chunk)])
    for i, m in enumerate(order):
        parts_in[share + i].wait()
        start(x_seconds.at[m], seconds.at[m])
    for copy in kv_in:
        copy.wait()
    for kv in kvs:
        start(kv_ref, kv.at[pl.ds(0, rows), :])
    lane = iota((rows, wide), 1)
    at = jnp.where(lane >= 3 * rows, lane - 3 * rows, lane)
    row = iota((rows, wide), 0)
    which = iota((16, wide), 0)
    tail_in.wait()
    bc_tail = bc_ref[rows - 16 :, :]
    for slot, extra in enumerate(extras):
        id_row = jnp.sum(jnp.where(at == row + rows * slot, column, 0.0), axis=0, keepdims=True)
        if slot == 0:
            extra[...] = jnp.where(which == 15, id_row, 0.0).astype(bf16)
        else:
            for part in range(2):
                s = 2 * (slot - 1) + part
                block = jnp.where(which == 15, id_row, 0.0)
                blocks = [
                    x_tail[:, s * piece + p * wide : s * piece + (p + 1) * wide].astype(f32)
                    for p in range(piece // wide)
                ]
                blocks.append(
                    jnp.concatenate(
                        [
                            bc_tail[:, s * states : (s + 1) * states].astype(f32),
                            bc_tail[:, (G + s) * states : (G + s + 1) * states].astype(f32),
                            jnp.broadcast_to(column[rows - 16 :, :], (16, 2 * LANES)),
                        ],
                        axis=1,
                    )
                )
                for i in range(3):
                    for p, source in enumerate(blocks):
                        block = jnp.where(which == 5 * i + p, source[13 + i : 14 + i, :], block)
                extra[16 * part : 16 * (part + 1), :] = block.astype(bf16)
        start(extra, kvs[slot].at[pl.ds(rows, extra.shape[0]), :])
    for copy in started[arriving:]:
        copy.wait()


def pick_halo(me, rows, mine, other):
    count = rows + 16
    second = count + rows
    third = second + rows + 32
    options = [
        other[second : second + 16, :],
        mine[second + 16 : second + 32, :],
        other[third : third + 16, :],
        mine[third + 16 : third + 32, :],
    ]
    picked = options[0].astype(f32)
    for j in range(1, 4):
        picked = jnp.where(me == j, options[j].astype(f32), picked)
    return jnp.where(lax.axis_index("ctx") >= 4, picked, 0.0)


def place_halo(scratch, picked, pieces):
    wide = picked.shape[1]
    for at, p in enumerate(pieces):
        which = iota((8, wide), 0)
        block = jnp.zeros((8, wide), f32)
        for i in range(3):
            block = jnp.where(which == 5 + i, picked[5 * i + p : 5 * i + p + 1, :], block)
        scratch[0:8, at * wide : (at + 1) * wide] = block


def conv_strip(src, columns, masks, taps):
    length = masks.shape[1]
    total = None
    for tap in range(4):
        term = taps[tap] * src[5 + tap : 5 + tap + length, columns]
        if tap < 3:
            term = term * masks[tap]
        total = term if total is None else total + term
    return (total * jax.nn.sigmoid(total)).astype(bf16)


def set_masks(masks, ids):
    length = masks.shape[1]
    own = ids[8 : 8 + length, :]
    for tap in range(3):
        masks[tap] = jnp.where(ids[5 + tap : 5 + tap + length, :] == own, 1.0, 0.0)


def taps_at(conv_ref, at):
    weights = conv_ref[:, pl.ds(pl.multiple_of(at, LANES), LANES)].astype(f32)
    return [weights[t : t + 1, :] for t in range(4)]


def one_hot(first, chunk):
    lane = iota((LANES, chunk), 0)
    head = iota((LANES, chunk), 1) // HD + first
    return jnp.where((lane % LOCAL_HEADS == head) & (lane < 3 * LOCAL_HEADS), 1.0, 0.0).astype(bf16)


def three_parts(value):
    lane = iota(value.shape, 1)
    high = value.astype(bf16).astype(f32)
    rest = value - high
    middle = rest.astype(bf16).astype(f32)
    low = rest - middle
    packed = jnp.where(
        lane < LOCAL_HEADS,
        high,
        jnp.where(
            lane < 2 * LOCAL_HEADS,
            pltpu.roll(middle, LOCAL_HEADS, 1),
            jnp.where(lane < 3 * LOCAL_HEADS, pltpu.roll(low, 2 * LOCAL_HEADS, 1), 0.0),
        ),
    )
    return packed.astype(bf16)


def conv_x_and_state(xs, masks, conv_ref, base, bcc, writes, first, xc_ref, state_ref):
    chunk = xc_ref.shape[1]
    for c in range(chunk // LANES):
        columns = slice(c * LANES, (c + 1) * LANES)
        xc_ref[:, columns] = conv_strip(xs, columns, masks, taps_at(conv_ref, base + c * LANES))
    factors = jnp.dot(writes, one_hot(first, chunk), preferred_element_type=f32)
    scaled = (xc_ref[...].astype(f32) * factors).astype(bf16)
    state = lax.dot_general(bcc, scaled, (((0,), (0,)), ((), ())), preferred_element_type=f32)
    state_ref[...] = state.astype(state_ref.dtype)


def turned(row, me):
    return pltpu.roll(
        jnp.broadcast_to(row, (8, LANES)), lax.rem(LANES - LOCAL_HEADS * me, LANES), 1
    )


def first_body(share, with_halo, *refs):
    pieces = refs[:share]
    convx, convbc, gains = refs[share : share + 3]
    rest = refs[share + 3 :]
    me = lax.rem(lax.axis_index("ctx"), share)
    if with_halo:
        picked = pick_halo(me, pieces[0].shape[0], rest[0], rest[1])
        rest = rest[2:]
    xc_o, bcc_o, state_o, ids_o, cum_o, step_o, writes_o, xs, bs, masks = rest
    chunk = xc_o.shape[1]
    piece = chunk * CHUNKS
    rows = pieces[0].shape[0]
    length = rows * share
    per_block = 4 * LANES
    if with_halo:
        place_halo(xs, picked, list(range(chunk // per_block)))
        place_halo(bs, picked, [4])
    else:
        xs[0:8, :] = jnp.zeros((8, chunk), f32)
        bs[0:8, :] = jnp.zeros((8, per_block), f32)
    for m in range(share):
        at = pl.multiple_of(8 + rows * (me ^ m), 8)
        xs[pl.ds(at, rows), :] = pieces[m][:, :chunk].astype(f32)
        bs[pl.ds(at, rows), : 3 * LANES] = pieces[m][:, chunk:].astype(f32)
    where_ids = 2 * LANES + LOCAL_HEADS
    ids_o[...] = jnp.broadcast_to(bs[:, where_ids : where_ids + 1], (length + 8, LANES))
    set_masks(masks, ids_o)
    for half in range(2):
        columns = slice(half * LANES, (half + 1) * LANES)
        taps = taps_at(convbc, half * G * LANES + me * LANES)
        bcc_o[:, columns] = conv_strip(bs, columns, masks, taps)
    raw = bs[8:, 2 * LANES : 3 * LANES] + turned(gains[0:1, :], me)[0:1, :]
    step = jnp.maximum(raw, 0.0) + jnp.log1p(jnp.exp(-jnp.abs(raw)))
    total = step * (-jnp.exp(turned(gains[1:2, :], me)[0:1, :]))
    row = iota((length, LANES), 0)
    reach = 1
    while reach < length:
        total = total + jnp.where(row >= reach, pltpu.roll(total, reach, 0), 0.0)
        reach *= 2
    own = ids_o[8:, :]
    last = length - 1
    writes = (
        jnp.where(own == own[last : last + 1, :], jnp.exp(total[last : last + 1, :] - total), 0.0)
        * step
    )
    cum_o[...] = total
    step_o[...] = step
    packed = three_parts(writes)
    writes_o[...] = packed
    conv_x_and_state(xs, masks, convx, me * piece, bcc_o[:, :LANES], packed, 0, xc_o, state_o)


def second_body(share, with_halo, *refs):
    pieces = refs[0]
    convx, bcc, ids, writes = refs[1:5]
    rest = refs[5:]
    me = lax.rem(lax.axis_index("ctx"), share)
    if with_halo:
        picked = pick_halo(me, pieces.shape[1], rest[0], rest[1])
        rest = rest[2:]
    xc_o, state_o, xs, masks = rest
    chunk = xc_o.shape[1]
    rows = pieces.shape[1]
    blocks = chunk // (4 * LANES)
    if with_halo:
        place_halo(xs, picked, list(range(blocks, 2 * blocks)))
    else:
        xs[0:8, :] = jnp.zeros((8, chunk), f32)
    for i in range(share):
        xs[8 + rows * i : 8 + rows * (i + 1), :] = pieces[i].astype(f32)
    set_masks(masks, ids)
    base = me * (chunk * CHUNKS) + chunk
    conv_x_and_state(
        xs, masks, convx, base, bcc[:, :LANES], writes[...], chunk // HD, xc_o, state_o
    )


def mixing_body(share, *refs):
    pieces, seconds = refs[:share], refs[share]
    xcs, refs = refs[share + 1 : share + 1 + CHUNKS], refs[share + 1 + CHUNKS :]
    mine, other, convx, convbc, bcc_in, cum, step, skip = refs[:8]
    rest = refs[8:]
    outs, (bcc, keep, head, head_ids, masks, first_x) = rest[:CHUNKS], rest[CHUNKS:]
    me = lax.rem(lax.axis_index("ctx"), share)
    length, chunk = xcs[0].shape
    rows = pieces[0].shape[0]
    piece = chunk * CHUNKS
    half = length // 2
    picked = pick_halo(me, rows, mine, other)
    place_halo(head, picked, list(range(5)))

    def first_rows(buffers, columns):
        start = buffers[0][:16, columns].astype(f32)
        for m in range(1, share):
            start = jnp.where(me == m, buffers[m][:16, columns].astype(f32), start)
        return start

    head[8:, :chunk] = first_rows(pieces, slice(0, chunk))
    head[8:, chunk:piece] = seconds[0, :16, :].astype(f32)
    head[8:, piece : piece + 3 * LANES] = first_rows(pieces, slice(chunk, chunk + 3 * LANES))
    where_ids = piece + 2 * LANES + LOCAL_HEADS
    head_ids[...] = jnp.broadcast_to(head[:, where_ids : where_ids + 1], (24, LANES))
    set_masks(masks, head_ids)
    for c in range(piece // LANES):
        columns = slice(c * LANES, (c + 1) * LANES)
        first_x[:, columns] = conv_strip(
            head, columns, masks, taps_at(convx, me * piece + c * LANES)
        )
    bcc[16:, :] = bcc_in[16:, :]
    for side in range(2):
        columns = slice(piece + side * LANES, piece + (side + 1) * LANES)
        taps = taps_at(convbc, side * G * LANES + me * LANES)
        bcc[:16, side * LANES : (side + 1) * LANES] = conv_strip(head, columns, masks, taps)

    inner = lax.dot_general(
        bcc[:, LANES:], bcc[:, :LANES], (((1,), (1,)), ((), ())), preferred_element_type=f32
    )
    ids = []
    for i in range(share):
        part = pieces[0][:, chunk + 2 * LANES :].astype(f32)
        for m in range(1, share):
            part = jnp.where((me ^ m) == i, pieces[m][:, chunk + 2 * LANES :].astype(f32), part)
        ids.append(part)
    ids = jnp.concatenate(ids, axis=0)
    across = ids.T[LOCAL_HEADS : LOCAL_HEADS + 1, :]
    own = jnp.broadcast_to(ids[:, LOCAL_HEADS : LOCAL_HEADS + 1], (length, length))
    allowed = (iota((length, length), 0) >= iota((length, length), 1)) & (own == across)
    inner = jnp.where(allowed, inner, 0.0)
    cums = cum[...]
    keep[...] = jnp.where(own[:, :LANES] == head_ids[7:8, :], jnp.exp(cums), 0.0)
    cum_rows = cums.T
    step_rows = step[...].T
    gains = three_parts(turned(skip[2:3, :], me))
    even = iota((half, LANES), 1) < HD
    for c in range(CHUNKS):
        first = c * (chunk // HD)
        spread = jnp.dot(gains, one_hot(first, chunk), preferred_element_type=f32)[0:1, :]
        for pair in range(chunk // LANES):
            columns = slice(pair * LANES, (pair + 1) * LANES)
            x_pair = jnp.concatenate(
                [
                    first_x[:, c * chunk + pair * LANES : c * chunk + (pair + 1) * LANES],
                    xcs[c][16:, columns],
                ],
                axis=0,
            )
            upper, lower = [], []
            for side in range(2):
                h = first + 2 * pair + side
                fade = cum_rows[h : h + 1, :]
                size = step_rows[h : h + 1, :]
                col = cums[:, h : h + 1]
                top = (
                    inner[:half, :half]
                    * (jnp.exp(jnp.minimum(col[:half] - fade[:, :half], 0.0)) * size[:, :half])
                ).astype(bf16)
                low = (
                    inner[half:, :] * (jnp.exp(jnp.minimum(col[half:] - fade, 0.0)) * size)
                ).astype(bf16)
                upper.append(jnp.dot(top, x_pair[:half, :], preferred_element_type=f32))
                lower.append(jnp.dot(low, x_pair, preferred_element_type=f32))
            gain = spread[:, columns]
            outs[c][:half, columns] = jnp.where(even, upper[0], upper[1]) + gain * x_pair[
                :half, :
            ].astype(f32)
            outs[c][half:, columns] = jnp.where(even, lower[0], lower[1]) + gain * x_pair[
                half:, :
            ].astype(f32)


def finish_body(share, first, state, bcc, keep, local, *rest):
    outs, total = rest[:-1], rest[-1]
    me = lax.rem(lax.axis_index("ctx"), share)
    chunk = local.shape[1]
    rows = outs[0].shape[-2]
    carried = jnp.dot(bcc[:, LANES:], state[...], preferred_element_type=f32)
    factors = jnp.dot(three_parts(keep[...]), one_hot(first, chunk), preferred_element_type=f32)
    total[...] = local[...] + carried * factors
    if len(outs) == 1:
        for i in range(share):
            outs[0][i] = total[rows * i : rows * (i + 1), :].astype(bf16)
        return
    for m in range(share):
        at = pl.multiple_of(rows * (me ^ m), rows)
        outs[m][...] = total[pl.ds(at, rows), :].astype(bf16)


def norm_body(share, *refs):
    z, gain, handed, out, handoff, buffer, sems = refs[-7:]
    me = lax.rem(lax.axis_index("ctx"), share)
    chunk = refs[0].shape[-1]
    parts, at = [], 0
    for whole in WHOLE:
        if whole:
            parts.append([lambda m, r=refs[at]: r[me ^ m]])
            at += 1
        else:
            parts.append([lambda m, r=refs[at : at + share]: r[m][...]])
            at += share
    piece = 2 * chunk
    copies = [pltpu.make_async_copy(handed, handoff, sems.at[share])]
    copies[0].start()
    for m in (0, 2, 3, 1):
        base = pl.multiple_of((me ^ m) * piece, LANES)
        gated = []
        for c, (source,) in enumerate(parts):
            gate = z[:, pl.ds(pl.multiple_of(base + c * chunk, LANES), chunk)].astype(f32)
            gated.append(source(m).astype(f32) * (gate * jax.nn.sigmoid(gate)))
        square = sum(jnp.sum(v * v, axis=1, keepdims=True) for v in gated)
        factor = lax.rsqrt(square / piece + norm_eps)
        for c, value in enumerate(gated):
            at = pl.ds(pl.multiple_of(base + c * chunk, LANES), chunk)
            buffer[m, :, c * chunk : (c + 1) * chunk] = (value * factor * gain[:, at]).astype(bf16)
        copies.append(
            pltpu.make_async_copy(buffer.at[m], out.at[:, pl.ds(base, piece)], sems.at[m])
        )
        copies[-1].start()
    for copy in copies:
        copy.wait()


def attention_body(q_ref, mine, other, out):
    rows = q_ref.shape[0]
    keys = 6 * rows
    ratio = AH // KVH
    heads_wide = KVH * HD
    here = lax.axis_index("ctx")
    odd = lax.rem(here, 2) == 1
    starts = (0, rows + 16, 2 * rows + 48)

    def id_rows(buffer):
        total = None
        for at in starts:
            row = buffer[at + rows : at + rows + 16, :].astype(f32)[15:16, :keys]
            total = row if total is None else total + row
        return total

    lane_row = iota((1, keys), 1)
    id_row = jnp.where(lane_row < 3 * rows, id_rows(mine), id_rows(other))
    own = mine[rows : rows + 16, :].astype(f32)[15:16, :rows]
    square = iota((rows, rows), 0) == iota((rows, rows), 1)
    column = jnp.sum(
        jnp.where(square, jnp.broadcast_to(own, (rows, rows)), 0.0), axis=1, keepdims=True
    )
    lane = iota((rows, keys), 1)
    earlier = (lane >= rows) | (lane <= iota((rows, keys), 0))
    sibling = (lane < 3 * rows) | (lane >= 4 * rows) | odd
    slot = lane % (3 * rows) // rows
    before = (slot == 0) | ((slot == 1) & (here >= 2)) | ((slot == 2) & (here >= 4))
    bias = jnp.where((id_row == column) & earlier & sibling & before, 0.0, -1e30)
    pairs = ratio // 2
    bias = jnp.concatenate([bias] * pairs, axis=0)
    even = iota((keys, LANES), 1) < HD
    even_out = iota((rows * pairs, LANES), 1) < HD

    def both(at, side):
        whole = jnp.concatenate(
            [b[s : s + rows, at : at + LANES] for b in (mine, other) for s in starts], axis=0
        ).astype(f32)
        kept = jnp.where(even == (side == 0), whole, 0.0)
        moved = pltpu.roll(kept, HD, 1)
        first, second = (kept, moved) if side == 0 else (moved, kept)
        return jnp.concatenate([first.astype(bf16), second.astype(bf16)], axis=0)

    for g in range(KVH):
        block = (g // 2) * LANES
        key_pair = both(block, g % 2)
        value_pair = both(heads_wide + block, g % 2)
        base = g * ratio * HD
        q = jnp.concatenate(
            [q_ref[:, base + i * LANES : base + (i + 1) * LANES] for i in range(pairs)], axis=0
        )
        scores = lax.dot_general(
            q, key_pair, (((1,), (1,)), ((), ())), preferred_element_type=f32
        ) * (1.0 / math.sqrt(HD))
        probs, totals = [], []
        for side in range(2):
            masked = scores[:, side * keys : (side + 1) * keys] + bias
            top = jnp.max(masked, axis=1, keepdims=True)
            weight = jnp.exp(masked - top)
            totals.append(jnp.sum(weight, axis=1, keepdims=True))
            probs.append(weight.astype(bf16))
        mixed = jnp.dot(
            jnp.concatenate(probs, axis=1), value_pair, preferred_element_type=f32
        ) / jnp.where(even_out, totals[0], totals[1])
        for i in range(pairs):
            out[:, base + i * LANES : base + (i + 1) * LANES] = mixed[
                i * rows : (i + 1) * rows, :
            ].astype(bf16)


def gathered_attention(query, keys, values, own_ids):
    tokens_here = query.shape[0]
    place = lax.axis_index("ctx")
    all_ids = lax.all_gather(own_ids, "ctx", axis=0, tiled=True)
    ratio = AH // KVH
    queries = query.reshape(tokens_here, KVH, ratio, HD)
    query_pos = place * tokens_here + jnp.arange(tokens_here)
    key_piece = lax.all_gather(keys, "ctx", axis=0, tiled=True)
    value_piece = lax.all_gather(values, "ctx", axis=0, tiled=True)
    count = key_piece.shape[0]
    width = math.gcd(count, 512)
    key_blocks = key_piece.reshape(count // width, width, KVH, HD)
    value_blocks = value_piece.reshape(count // width, width, KVH, HD)
    shape = (KVH, ratio, tokens_here)

    def visit(running, item):
        key_block, value_block, order = item
        first = order * width
        key_ids = lax.dynamic_slice_in_dim(all_ids, first, width)
        key_pos = first + jnp.arange(width)
        allowed = (query_pos[:, None] >= key_pos[None, :]) & (own_ids[:, None] == key_ids[None, :])
        largest, totals, accum = running
        logits = jnp.einsum(
            "tgrd,mgd->grtm", queries, key_block, preferred_element_type=f32
        ) / math.sqrt(HD)
        masked = jnp.where(allowed, logits, -1e30)
        newest = jnp.maximum(largest, jnp.max(masked, axis=-1))
        weight = jnp.where(allowed, jnp.exp(masked - newest[..., None]), 0.0)
        correct = jnp.exp(largest - newest)
        totals = totals * correct + jnp.sum(weight, axis=-1)
        accum = accum * correct[..., None] + jnp.einsum(
            "grtm,mgd->grtd", weight.astype(bf16), value_block, preferred_element_type=f32
        )
        return (newest, totals, accum), None

    start = (jnp.full(shape, -1e30, f32), jnp.zeros(shape, f32), jnp.zeros(shape + (HD,), f32))
    (_, totals, accum), _ = lax.scan(
        visit, start, (key_blocks, value_blocks, jnp.arange(count // width, dtype=jnp.int32))
    )
    attended = accum / totals[..., None]
    return jnp.transpose(attended, (2, 0, 1, 3)).reshape(tokens_here, AH * HD).astype(bf16)


def on_device(
    x_in,
    z_in,
    bc_in,
    dt_raw,
    a_log,
    dt_bias,
    d_skip,
    conv_x,
    conv_bc,
    norm_gain,
    seg_ids,
    query,
    keys,
    values,
):
    ranks = lax.axis_size("ctx")
    rows, width = x_in.shape[1:]
    share = BLK // rows
    blocks = ranks // share
    piece = width // share
    chunk = piece // CHUNKS
    reach = -(-(rows * ranks // 2 - 1) // rows)
    shape = jax.ShapeDtypeStruct
    state_type = bf16 if blocks <= 2 else f32

    wide = 4 * LANES
    packed = call(
        functools.partial(pack_body, share),
        [shape((rows, chunk + 3 * LANES), bf16)] * share
        + [shape((share, rows, chunk), bf16)]
        + [shape((rows + 16, wide), bf16)]
        + [shape((rows + 32, wide), bf16)] * 2,
        scratch=[
            pltpu.VMEM((rows, LANES), bf16),
            pltpu.VMEM((rows, bc_in.shape[2]), bf16),
            pltpu.VMEM((share, rows, chunk), bf16),
            pltpu.VMEM((share, rows, chunk), bf16),
            pltpu.VMEM((rows, wide), bf16),
            pltpu.VMEM((share, rows, 3 * LANES), bf16),
            pltpu.VMEM((16, wide), bf16),
            pltpu.VMEM((32, wide), bf16),
            pltpu.VMEM((32, wide), bf16),
            pltpu.VMEM((16, width), bf16),
            pltpu.SemaphoreType.DMA((5 * share + 11,)),
        ],
        in_specs=[hbm()] * 3 + [vmem()] + [hbm()] * 2,
        out_specs=[hbm()] * (share + 4),
        room=PACK_ROOM,
        bytes_accessed=5 * 2**20,
    )(x_in[0], bc_in[0], dt_raw[0], seg_ids, keys[0], values[0])
    send, send_b, (kv_own, kv_near, kv_far) = packed[:share], packed[share], packed[share + 1 :]
    order = [2, 3, 1]

    def exchanged(values):
        here = {0: values[0]}
        for m in order:
            here[m] = crossed(values[m], "ctx", m)
        return [here[m] for m in range(share)]

    pieces = exchanged(send)
    near, far = turned_on(kv_near, "ctx", 2), turned_on(kv_far, "ctx", 4)
    send_b, pieces[2] = lax.optimization_barrier((send_b, pieces[2]))
    groups = [[b * share + i for i in range(share)] for b in range(blocks)]
    pieces_b = lax.all_to_all(send_b, "ctx", 0, 0, tiled=True, axis_index_groups=groups)
    halo = []
    if blocks > 2:
        mine = jnp.concatenate([kv_own, near, far], axis=0)
        other = crossed(mine, "ctx", 1)
        halo = [mine, other]
    per_token = shape((BLK, LANES), f32)
    head_gains = jnp.concatenate([dt_bias, a_log, d_skip], axis=0)
    xc_a, bcc_first, state_a, ids_col, cum, step, writes = call(
        functools.partial(first_body, share, blocks > 2),
        [
            shape((BLK, chunk), bf16),
            shape((BLK, 2 * LANES), bf16),
            shape((LANES, chunk), state_type),
            shape((BLK + 8, LANES), f32),
            per_token,
            per_token,
            shape((BLK, LANES), bf16),
        ],
        scratch=[
            pltpu.VMEM((BLK + 8, chunk), f32),
            pltpu.VMEM((BLK + 8, wide), f32),
            pltpu.VMEM((3, BLK, LANES), f32),
        ],
        flops=0,
        bytes_accessed=1024,
    )(*pieces, conv_x[0], conv_bc[0], head_gains, *halo)
    if blocks <= 2:
        near, far, cum = lax.optimization_barrier((near, far, cum))
        mine = jnp.concatenate([kv_own, near, far], axis=0)
        other = crossed(mine, "ctx", 1)
    xc_b, state_b = call(
        functools.partial(second_body, share, blocks > 2),
        [shape((BLK, chunk), bf16), shape((LANES, chunk), state_type)],
        scratch=[pltpu.VMEM((BLK + 8, chunk), f32), pltpu.VMEM((3, BLK, LANES), f32)],
        flops=2**28,
        bytes_accessed=3 * 2**20,
    )(pieces_b, conv_x[0], bcc_first, ids_col, writes, *halo)
    per_head = chunk // HD

    def entering(state, first):
        if blocks > 2:
            same = ids_col[BLK + 7, :] == ids_col[7, :]
            fade = jnp.where(same, jnp.exp(cum[BLK - 1, :]), 0.0)[first : first + per_head]
            fade = jnp.repeat(fade, HD)[None, :]
            far = 1
            while far < blocks:
                came = shifted(state, "ctx", far * share)
                came_fade = shifted(fade, "ctx", far * share)
                state = state + fade * came
                fade = fade * came_fade
                far *= 2
        return turned_on(state, "ctx", share).astype(bf16)

    entry_a = entering(state_a, 0)
    entry_b = entering(state_b, per_head)

    local_a, local_b, bcc, keep = call(
        functools.partial(mixing_body, share),
        [shape((BLK, chunk), f32)] * CHUNKS + [shape((BLK, 2 * LANES), bf16), per_token],
        scratch=[
            pltpu.VMEM((24, piece + wide), f32),
            pltpu.VMEM((24, LANES), f32),
            pltpu.VMEM((3, 16, LANES), f32),
            pltpu.VMEM((16, piece), bf16),
        ],
        flops=2**31,
        bytes_accessed=4 * 2**20,
    )(*pieces, pieces_b, xc_a, xc_b, mine, other, conv_x[0], conv_bc[0], bcc_first, cum, step, head_gains)

    if reach <= share:
        attended = call(
            attention_body,
            shape((rows, AH * HD), bf16),
            flops=2**30,
            bytes_accessed=2**20,
        )(query[0], mine, other)
    else:
        attended = gathered_attention(query[0], keys[0], values[0], seg_ids[0])
    local_a, attended = lax.optimization_barrier((local_a, attended))
    handoff = turned_on(attended, "pipe", 1)

    sent = []
    for c, (entry, local) in enumerate(((entry_a, local_a), (entry_b, local_b))):
        y = call(
            functools.partial(finish_body, share, c * per_head),
            [shape((share, rows, chunk), bf16)] if WHOLE[c] else [shape((rows, chunk), bf16)] * share,
            scratch=[pltpu.VMEM((BLK, chunk), f32)],
            flops=2**28,
            bytes_accessed=2 * 2**20,
        )(entry, bcc, keep, local)
        if WHOLE[c]:
            groups = [[b * share + i for i in range(share)] for b in range(blocks)]
            sent.append(
                lax.all_to_all(y[0], "ctx", 0, 0, tiled=True, axis_index_groups=groups)
            )
            continue
        sent += exchanged(y)
    mamba_out, handoff = call(
        functools.partial(norm_body, share),
        [shape((rows, width), bf16), shape((rows, AH * HD), bf16)],
        scratch=[pltpu.VMEM((share, rows, piece), bf16), pltpu.SemaphoreType.DMA((share + 1,))],
        out_specs=[hbm()] * 2,
        bytes_accessed=3 * 2**20,
    )(*sent, z_in[0], norm_gain, handoff)
    return (mamba_out[None], handoff[None])


def solution(mesh):
    in_specs = (
        P("pipe", "ctx", None),
        P("pipe", "ctx", None),
        P("pipe", "ctx", None),
        P("pipe", "ctx", None),
        P("pipe", None),
        P("pipe", None),
        P("pipe", None),
        P("pipe", None, None),
        P("pipe", None, None),
        P("pipe", None),
        P("pipe", "ctx"),
        P("pipe", "ctx", None),
        P("pipe", "ctx", None),
        P("pipe", "ctx", None),
    )
    out_specs = (P("pipe", "ctx", None), P("pipe", "ctx", None))
    return jax.shard_map(
        on_device, mesh=mesh, in_specs=in_specs, out_specs=out_specs, check_vma=False
    )
```

```python
import functools
import math

import jax
import jax.numpy as jnp
from jax import lax
from jax.experimental import pallas as pl
from jax.experimental.pallas import tpu as pltpu
from jax.sharding import PartitionSpec as P

G = 4
AH = 32
KVH = 4
HD = 64
BLK = 256
LANES = 128
LOCAL_HEADS = 32
CHUNKS = 2
PACK_ROOM = 58
WHOLE = (False, False)

norm_eps = 1e-05
bf16 = jnp.bfloat16
f32 = jnp.float32


def shifted(value, axis, steps):
    count = lax.axis_size(axis)
    return lax.ppermute(value, axis, [(i, i + steps) for i in range(count - steps)])


def turned_on(value, axis, steps):
    count = lax.axis_size(axis)
    return lax.ppermute(value, axis, [(i, (i + steps) % count) for i in range(count)])


def crossed(value, axis, mask):
    count = lax.axis_size(axis)
    return lax.ppermute(value, axis, [(i, i ^ mask) for i in range(count)])


def iota(shape, dim):
    return lax.broadcasted_iota(jnp.int32, shape, dim)


def call(body, outs, scratch=(), flops=0, bytes_accessed=0, room=48, **specs):
    return pl.pallas_call(
        body,
        out_shape=outs,
        scratch_shapes=list(scratch),
        compiler_params=pltpu.CompilerParams(vmem_limit_bytes=int(room * 2**20)),
        cost_estimate=pl.CostEstimate(
            flops=flops, bytes_accessed=bytes_accessed, transcendentals=0
        ),
        **specs,
    )


def hbm():
    return pl.BlockSpec(memory_space=pltpu.HBM)


def vmem():
    return pl.BlockSpec(memory_space=pltpu.VMEM)


def pack_body(share, x_hbm, bc_hbm, dt_hbm, ids_ref, k_hbm, v_hbm, *refs):
    sends, seconds = refs[:share], refs[share]
    kvs, rest = refs[share + 1 : share + 4], refs[share + 4 :]
    dt_ref, bc_ref, x_firsts, x_seconds, kv_ref, marks, own_extra, near_extra, far_extra = rest[:-2]
    x_tail, sems = rest[-2:]
    extras = (own_extra, near_extra, far_extra)
    me = lax.rem(lax.axis_index("ctx"), share)
    rows, width = x_hbm.shape
    piece = width // share
    chunk = piece // CHUNKS
    states = bc_hbm.shape[1] // (2 * G)
    wide = 4 * LANES
    started = []

    def start(source, target):
        copy = pltpu.make_async_copy(source, target, sems.at[len(started)])
        copy.start()
        started.append(copy)
        return copy

    order = (2, 3, 1, 0)
    steps_in, small_in = start(dt_hbm, dt_ref), start(bc_hbm, bc_ref)
    parts_in = []
    for c, held in enumerate((x_firsts, x_seconds)):
        for m in order:
            at = pl.multiple_of((me ^ m) * piece + c * chunk, LANES)
            if c == 0:
                parts_in.append(start(x_hbm.at[:, pl.ds(at, chunk)], held.at[m]))
            else:
                at = m * piece + chunk
                parts_in.append(start(x_hbm.at[:, pl.ds(at, chunk)], held.at[m]))
    kv_in = [
        start(source, kv_ref.at[:, pl.ds(side * wide // 2, wide // 2)])
        for side, source in enumerate((k_hbm, v_hbm))
    ]
    tail_in = start(x_hbm.at[pl.ds(rows - 16, 16), :], x_tail)
    arriving = len(started)
    number = ids_ref[...].astype(f32) + 1.0
    square = iota((rows, rows), 0) == iota((rows, rows), 1)
    column = jnp.sum(
        jnp.where(square, jnp.broadcast_to(number, (rows, rows)), 0.0), axis=1, keepdims=True
    )
    small = iota((rows, LANES), 1)
    steps_in.wait()
    steps = dt_ref[...].astype(f32)
    small_in.wait()
    for m in order:
        s = me ^ m
        turn = lax.rem(LANES - LOCAL_HEADS * s, LANES)
        marked = jnp.where(small < LOCAL_HEADS, pltpu.roll(steps, turn, 1), column).astype(bf16)
        for side in range(2):
            at = pl.multiple_of((side * G + s) * states, LANES)
            marks[m, :, side * states : (side + 1) * states] = bc_ref[:, pl.ds(at, states)]
        marks[m, :, 2 * states :] = marked
        start(marks.at[m], sends[m].at[:, pl.ds(chunk, 2 * states + LANES)])
    for i, m in enumerate(order):
        parts_in[i].wait()
        start(x_firsts.at[m], sends[m].at[:, pl.ds(0, chunk)])
    for i, m in enumerate(order):
        parts_in[share + i].wait()
        start(x_seconds.at[m], seconds.at[m])
    for copy in kv_in:
        copy.wait()
    for kv in kvs:
        start(kv_ref, kv.at[pl.ds(0, rows), :])
    lane = iota((rows, wide), 1)
    at = jnp.where(lane >= 3 * rows, lane - 3 * rows, lane)
    row = iota((rows, wide), 0)
    which = iota((16, wide), 0)
    tail_in.wait()
    bc_tail = bc_ref[rows - 16 :, :]
    for slot, extra in enumerate(extras):
        id_row = jnp.sum(jnp.where(at == row + rows * slot, column, 0.0), axis=0, keepdims=True)
        if slot == 0:
            extra[...] = jnp.where(which == 15, id_row, 0.0).astype(bf16)
        else:
            for part in range(2):
                s = 2 * (slot - 1) + part
                block = jnp.where(which == 15, id_row, 0.0)
                blocks = [
                    x_tail[:, s * piece + p * wide : s * piece + (p + 1) * wide].astype(f32)
                    for p in range(piece // wide)
                ]
                blocks.append(
                    jnp.concatenate(
                        [
                            bc_tail[:, s * states : (s + 1) * states].astype(f32),
                            bc_tail[:, (G + s) * states : (G + s + 1) * states].astype(f32),
                            jnp.broadcast_to(column[rows - 16 :, :], (16, 2 * LANES)),
                        ],
                        axis=1,
                    )
                )
                for i in range(3):
                    for p, source in enumerate(blocks):
                        block = jnp.where(which == 5 * i + p, source[13 + i : 14 + i, :], block)
                extra[16 * part : 16 * (part + 1), :] = block.astype(bf16)
        start(extra, kvs[slot].at[pl.ds(rows, extra.shape[0]), :])
    for copy in started[arriving:]:
        copy.wait()


def pick_halo(me, rows, mine, other):
    count = rows + 16
    second = count + rows
    third = second + rows + 32
    options = [
        other[second : second + 16, :],
        mine[second + 16 : second + 32, :],
        other[third : third + 16, :],
        mine[third + 16 : third + 32, :],
    ]
    picked = options[0].astype(f32)
    for j in range(1, 4):
        picked = jnp.where(me == j, options[j].astype(f32), picked)
    return jnp.where(lax.axis_index("ctx") >= 4, picked, 0.0)


def place_halo(scratch, picked, pieces):
    wide = picked.shape[1]
    for at, p in enumerate(pieces):
        which = iota((8, wide), 0)
        block = jnp.zeros((8, wide), f32)
        for i in range(3):
            block = jnp.where(which == 5 + i, picked[5 * i + p : 5 * i + p + 1, :], block)
        scratch[0:8, at * wide : (at + 1) * wide] = block


def conv_strip(src, columns, masks, taps):
    length = masks.shape[1]
    total = None
    for tap in range(4):
        term = taps[tap] * src[5 + tap : 5 + tap + length, columns]
        if tap < 3:
            term = term * masks[tap]
        total = term if total is None else total + term
    return (total * jax.nn.sigmoid(total)).astype(bf16)


def set_masks(masks, ids):
    length = masks.shape[1]
    own = ids[8 : 8 + length, :]
    for tap in range(3):
        masks[tap] = jnp.where(ids[5 + tap : 5 + tap + length, :] == own, 1.0, 0.0)


def taps_at(conv_ref, at):
    weights = conv_ref[:, pl.ds(pl.multiple_of(at, LANES), LANES)].astype(f32)
    return [weights[t : t + 1, :] for t in range(4)]


def one_hot(first, chunk):
    lane = iota((LANES, chunk), 0)
    head = iota((LANES, chunk), 1) // HD + first
    return jnp.where((lane % LOCAL_HEADS == head) & (lane < 3 * LOCAL_HEADS), 1.0, 0.0).astype(bf16)


def three_parts(value):
    lane = iota(value.shape, 1)
    high = value.astype(bf16).astype(f32)
    rest = value - high
    middle = rest.astype(bf16).astype(f32)
    low = rest - middle
    packed = jnp.where(
        lane < LOCAL_HEADS,
        high,
        jnp.where(
            lane < 2 * LOCAL_HEADS,
            pltpu.roll(middle, LOCAL_HEADS, 1),
            jnp.where(lane < 3 * LOCAL_HEADS, pltpu.roll(low, 2 * LOCAL_HEADS, 1), 0.0),
        ),
    )
    return packed.astype(bf16)


def conv_x_and_state(xs, masks, conv_ref, base, bcc, writes, first, xc_ref, state_ref):
    chunk = xc_ref.shape[1]
    for c in range(chunk // LANES):
        columns = slice(c * LANES, (c + 1) * LANES)
        xc_ref[:, columns] = conv_strip(xs, columns, masks, taps_at(conv_ref, base + c * LANES))
    factors = jnp.dot(writes, one_hot(first, chunk), preferred_element_type=f32)
    scaled = (xc_ref[...].astype(f32) * factors).astype(bf16)
    state = lax.dot_general(bcc, scaled, (((0,), (0,)), ((), ())), preferred_element_type=f32)
    state_ref[...] = state.astype(state_ref.dtype)


def turned(row, me):
    return pltpu.roll(
        jnp.broadcast_to(row, (8, LANES)), lax.rem(LANES - LOCAL_HEADS * me, LANES), 1
    )


def decays(marks, gains, me):
    length = marks.shape[0]
    raw = marks + turned(gains[0:1, :], me)[0:1, :]
    step = jnp.maximum(raw, 0.0) + jnp.log1p(jnp.exp(-jnp.abs(raw)))
    total = step * (-jnp.exp(turned(gains[1:2, :], me)[0:1, :]))
    row = iota((length, LANES), 0)
    reach = 1
    while reach < length:
        total = total + jnp.where(row >= reach, pltpu.roll(total, reach, 0), 0.0)
        reach *= 2
    return step, total


def first_body(share, with_halo, *refs):
    pieces = refs[:share]
    convx, convbc, gains = refs[share : share + 3]
    rest = refs[share + 3 :]
    me = lax.rem(lax.axis_index("ctx"), share)
    if with_halo:
        picked = pick_halo(me, pieces[0].shape[0], rest[0], rest[1])
        rest = rest[2:]
    xc_o, bcc_o, state_o, ids_o, writes_o, *decay_o, xs, bs, masks = rest
    chunk = xc_o.shape[1]
    piece = chunk * CHUNKS
    rows = pieces[0].shape[0]
    length = rows * share
    per_block = 4 * LANES
    if with_halo:
        place_halo(xs, picked, list(range(chunk // per_block)))
        place_halo(bs, picked, [4])
    else:
        xs[0:8, :] = jnp.zeros((8, chunk), f32)
        bs[0:8, :] = jnp.zeros((8, per_block), f32)
    for m in range(share):
        at = pl.multiple_of(8 + rows * (me ^ m), 8)
        xs[pl.ds(at, rows), :] = pieces[m][:, :chunk].astype(f32)
        bs[pl.ds(at, rows), : 3 * LANES] = pieces[m][:, chunk:].astype(f32)
    where_ids = 2 * LANES + LOCAL_HEADS
    ids_o[...] = jnp.broadcast_to(bs[:, where_ids : where_ids + 1], (length + 8, LANES))
    set_masks(masks, ids_o)
    for half in range(2):
        columns = slice(half * LANES, (half + 1) * LANES)
        taps = taps_at(convbc, half * G * LANES + me * LANES)
        bcc_o[:, columns] = conv_strip(bs, columns, masks, taps)
    step, total = decays(bs[8:, 2 * LANES : 3 * LANES], gains, me)
    own = ids_o[8:, :]
    last = length - 1
    writes = (
        jnp.where(own == own[last : last + 1, :], jnp.exp(total[last : last + 1, :] - total), 0.0)
        * step
    )
    for fade in decay_o:
        fade[...] = jnp.broadcast_to(jnp.exp(total[last : last + 1, :]), (8, LANES))
    packed = three_parts(writes)
    writes_o[...] = packed
    conv_x_and_state(xs, masks, convx, me * piece, bcc_o[:, :LANES], packed, 0, xc_o, state_o)


def second_body(share, with_halo, *refs):
    pieces = refs[0]
    convx, bcc, ids, writes = refs[1:5]
    rest = refs[5:]
    me = lax.rem(lax.axis_index("ctx"), share)
    if with_halo:
        picked = pick_halo(me, pieces.shape[1], rest[0], rest[1])
        rest = rest[2:]
    xc_o, state_o, xs, masks = rest
    chunk = xc_o.shape[1]
    rows = pieces.shape[1]
    blocks = chunk // (4 * LANES)
    if with_halo:
        place_halo(xs, picked, list(range(blocks, 2 * blocks)))
    else:
        xs[0:8, :] = jnp.zeros((8, chunk), f32)
    for i in range(share):
        xs[8 + rows * i : 8 + rows * (i + 1), :] = pieces[i].astype(f32)
    set_masks(masks, ids)
    base = me * (chunk * CHUNKS) + chunk
    conv_x_and_state(
        xs, masks, convx, base, bcc[:, :LANES], writes[...], chunk // HD, xc_o, state_o
    )


def mixing_body(share, *refs):
    pieces, seconds = refs[:share], refs[share]
    xcs, refs = refs[share + 1 : share + 1 + CHUNKS], refs[share + 1 + CHUNKS :]
    mine, other, convx, convbc, bcc_in, skip = refs[:6]
    rest = refs[6:]
    outs, (bcc, keep, head, head_ids, masks, first_x) = rest[:CHUNKS], rest[CHUNKS:]
    me = lax.rem(lax.axis_index("ctx"), share)
    length, chunk = xcs[0].shape
    rows = pieces[0].shape[0]
    piece = chunk * CHUNKS
    half = length // 2
    picked = pick_halo(me, rows, mine, other)
    place_halo(head, picked, list(range(5)))

    def first_rows(buffers, columns):
        start = buffers[0][:16, columns].astype(f32)
        for m in range(1, share):
            start = jnp.where(me == m, buffers[m][:16, columns].astype(f32), start)
        return start

    head[8:, :chunk] = first_rows(pieces, slice(0, chunk))
    head[8:, chunk:piece] = seconds[0, :16, :].astype(f32)
    head[8:, piece : piece + 3 * LANES] = first_rows(pieces, slice(chunk, chunk + 3 * LANES))
    where_ids = piece + 2 * LANES + LOCAL_HEADS
    head_ids[...] = jnp.broadcast_to(head[:, where_ids : where_ids + 1], (24, LANES))
    set_masks(masks, head_ids)
    for c in range(piece // LANES):
        columns = slice(c * LANES, (c + 1) * LANES)
        first_x[:, columns] = conv_strip(
            head, columns, masks, taps_at(convx, me * piece + c * LANES)
        )
    bcc[16:, :] = bcc_in[16:, :]
    for side in range(2):
        columns = slice(piece + side * LANES, piece + (side + 1) * LANES)
        taps = taps_at(convbc, side * G * LANES + me * LANES)
        bcc[:16, side * LANES : (side + 1) * LANES] = conv_strip(head, columns, masks, taps)

    inner = lax.dot_general(
        bcc[:, LANES:], bcc[:, :LANES], (((1,), (1,)), ((), ())), preferred_element_type=f32
    )
    ids = []
    for i in range(share):
        part = pieces[0][:, chunk + 2 * LANES :].astype(f32)
        for m in range(1, share):
            part = jnp.where((me ^ m) == i, pieces[m][:, chunk + 2 * LANES :].astype(f32), part)
        ids.append(part)
    ids = jnp.concatenate(ids, axis=0)
    across = ids.T[LOCAL_HEADS : LOCAL_HEADS + 1, :]
    own = jnp.broadcast_to(ids[:, LOCAL_HEADS : LOCAL_HEADS + 1], (length, length))
    allowed = (iota((length, length), 0) >= iota((length, length), 1)) & (own == across)
    inner = jnp.where(allowed, inner, 0.0)
    step, cums = decays(ids, skip, me)
    keep[...] = jnp.where(own[:, :LANES] == head_ids[7:8, :], jnp.exp(cums), 0.0)
    cum_rows = cums.T
    step_rows = step.T
    gains = three_parts(turned(skip[2:3, :], me))
    even = iota((half, LANES), 1) < HD
    for c in range(CHUNKS):
        first = c * (chunk // HD)
        spread = jnp.dot(gains, one_hot(first, chunk), preferred_element_type=f32)[0:1, :]
        for pair in range(chunk // LANES):
            columns = slice(pair * LANES, (pair + 1) * LANES)
            x_pair = jnp.concatenate(
                [
                    first_x[:, c * chunk + pair * LANES : c * chunk + (pair + 1) * LANES],
                    xcs[c][16:, columns],
                ],
                axis=0,
            )
            upper, lower = [], []
            for side in range(2):
                h = first + 2 * pair + side
                fade = cum_rows[h : h + 1, :]
                size = step_rows[h : h + 1, :]
                col = cums[:, h : h + 1]
                top = (
                    inner[:half, :half]
                    * (jnp.exp(jnp.minimum(col[:half] - fade[:, :half], 0.0)) * size[:, :half])
                ).astype(bf16)
                low = (
                    inner[half:, :] * (jnp.exp(jnp.minimum(col[half:] - fade, 0.0)) * size)
                ).astype(bf16)
                upper.append(jnp.dot(top, x_pair[:half, :], preferred_element_type=f32))
                lower.append(jnp.dot(low, x_pair, preferred_element_type=f32))
            gain = spread[:, columns]
            outs[c][:half, columns] = jnp.where(even, upper[0], upper[1]) + gain * x_pair[
                :half, :
            ].astype(f32)
            outs[c][half:, columns] = jnp.where(even, lower[0], lower[1]) + gain * x_pair[
                half:, :
            ].astype(f32)


def finish_body(share, first, state, bcc, keep, local, *rest):
    outs, total = rest[:-1], rest[-1]
    me = lax.rem(lax.axis_index("ctx"), share)
    chunk = local.shape[1]
    rows = outs[0].shape[-2]
    carried = jnp.dot(bcc[:, LANES:], state[...], preferred_element_type=f32)
    factors = jnp.dot(three_parts(keep[...]), one_hot(first, chunk), preferred_element_type=f32)
    total[...] = local[...] + carried * factors
    if len(outs) == 1:
        for i in range(share):
            outs[0][i] = total[rows * i : rows * (i + 1), :].astype(bf16)
        return
    for m in range(share):
        at = pl.multiple_of(rows * (me ^ m), rows)
        outs[m][...] = total[pl.ds(at, rows), :].astype(bf16)


def norm_body(share, *refs):
    z, gain, handed, out, handoff, buffer, sems = refs[-7:]
    me = lax.rem(lax.axis_index("ctx"), share)
    chunk = refs[0].shape[-1]
    parts, at = [], 0
    for whole in WHOLE:
        if whole:
            parts.append([lambda m, r=refs[at]: r[me ^ m]])
            at += 1
        else:
            parts.append([lambda m, r=refs[at : at + share]: r[m][...]])
            at += share
    piece = 2 * chunk
    copies = [pltpu.make_async_copy(handed, handoff, sems.at[share])]
    copies[0].start()
    for m in (0, 2, 3, 1):
        base = pl.multiple_of((me ^ m) * piece, LANES)
        gated = []
        for c, (source,) in enumerate(parts):
            gate = z[:, pl.ds(pl.multiple_of(base + c * chunk, LANES), chunk)].astype(f32)
            gated.append(source(m).astype(f32) * (gate * jax.nn.sigmoid(gate)))
        square = sum(jnp.sum(v * v, axis=1, keepdims=True) for v in gated)
        factor = lax.rsqrt(square / piece + norm_eps)
        for c, value in enumerate(gated):
            at = pl.ds(pl.multiple_of(base + c * chunk, LANES), chunk)
            buffer[m, :, c * chunk : (c + 1) * chunk] = (value * factor * gain[:, at]).astype(bf16)
        copies.append(
            pltpu.make_async_copy(buffer.at[m], out.at[:, pl.ds(base, piece)], sems.at[m])
        )
        copies[-1].start()
    for copy in copies:
        copy.wait()


def attention_body(q_ref, mine, other, out):
    rows = q_ref.shape[0]
    keys = 6 * rows
    ratio = AH // KVH
    heads_wide = KVH * HD
    here = lax.axis_index("ctx")
    odd = lax.rem(here, 2) == 1
    starts = (0, rows + 16, 2 * rows + 48)

    def id_rows(buffer):
        total = None
        for at in starts:
            row = buffer[at + rows : at + rows + 16, :].astype(f32)[15:16, :keys]
            total = row if total is None else total + row
        return total

    lane_row = iota((1, keys), 1)
    id_row = jnp.where(lane_row < 3 * rows, id_rows(mine), id_rows(other))
    own = mine[rows : rows + 16, :].astype(f32)[15:16, :rows]
    square = iota((rows, rows), 0) == iota((rows, rows), 1)
    column = jnp.sum(
        jnp.where(square, jnp.broadcast_to(own, (rows, rows)), 0.0), axis=1, keepdims=True
    )
    lane = iota((rows, keys), 1)
    earlier = (lane >= rows) | (lane <= iota((rows, keys), 0))
    sibling = (lane < 3 * rows) | (lane >= 4 * rows) | odd
    slot = lane % (3 * rows) // rows
    before = (slot == 0) | ((slot == 1) & (here >= 2)) | ((slot == 2) & (here >= 4))
    bias = jnp.where((id_row == column) & earlier & sibling & before, 0.0, -1e30)
    pairs = ratio // 2
    bias = jnp.concatenate([bias] * pairs, axis=0)
    even = iota((keys, LANES), 1) < HD
    even_out = iota((rows * pairs, LANES), 1) < HD

    def both(at, side):
        whole = jnp.concatenate(
            [b[s : s + rows, at : at + LANES] for b in (mine, other) for s in starts], axis=0
        ).astype(f32)
        kept = jnp.where(even == (side == 0), whole, 0.0)
        moved = pltpu.roll(kept, HD, 1)
        first, second = (kept, moved) if side == 0 else (moved, kept)
        return jnp.concatenate([first.astype(bf16), second.astype(bf16)], axis=0)

    for g in range(KVH):
        block = (g // 2) * LANES
        key_pair = both(block, g % 2)
        value_pair = both(heads_wide + block, g % 2)
        base = g * ratio * HD
        q = jnp.concatenate(
            [q_ref[:, base + i * LANES : base + (i + 1) * LANES] for i in range(pairs)], axis=0
        )
        scores = lax.dot_general(
            q, key_pair, (((1,), (1,)), ((), ())), preferred_element_type=f32
        ) * (1.0 / math.sqrt(HD))
        probs, totals = [], []
        for side in range(2):
            masked = scores[:, side * keys : (side + 1) * keys] + bias
            top = jnp.max(masked, axis=1, keepdims=True)
            weight = jnp.exp(masked - top)
            totals.append(jnp.sum(weight, axis=1, keepdims=True))
            probs.append(weight.astype(bf16))
        mixed = jnp.dot(
            jnp.concatenate(probs, axis=1), value_pair, preferred_element_type=f32
        ) / jnp.where(even_out, totals[0], totals[1])
        for i in range(pairs):
            out[:, base + i * LANES : base + (i + 1) * LANES] = mixed[
                i * rows : (i + 1) * rows, :
            ].astype(bf16)


def gathered_attention(query, keys, values, own_ids):
    tokens_here = query.shape[0]
    place = lax.axis_index("ctx")
    all_ids = lax.all_gather(own_ids, "ctx", axis=0, tiled=True)
    ratio = AH // KVH
    queries = query.reshape(tokens_here, KVH, ratio, HD)
    query_pos = place * tokens_here + jnp.arange(tokens_here)
    key_piece = lax.all_gather(keys, "ctx", axis=0, tiled=True)
    value_piece = lax.all_gather(values, "ctx", axis=0, tiled=True)
    count = key_piece.shape[0]
    width = math.gcd(count, 512)
    key_blocks = key_piece.reshape(count // width, width, KVH, HD)
    value_blocks = value_piece.reshape(count // width, width, KVH, HD)
    shape = (KVH, ratio, tokens_here)

    def visit(running, item):
        key_block, value_block, order = item
        first = order * width
        key_ids = lax.dynamic_slice_in_dim(all_ids, first, width)
        key_pos = first + jnp.arange(width)
        allowed = (query_pos[:, None] >= key_pos[None, :]) & (own_ids[:, None] == key_ids[None, :])
        largest, totals, accum = running
        logits = jnp.einsum(
            "tgrd,mgd->grtm", queries, key_block, preferred_element_type=f32
        ) / math.sqrt(HD)
        masked = jnp.where(allowed, logits, -1e30)
        newest = jnp.maximum(largest, jnp.max(masked, axis=-1))
        weight = jnp.where(allowed, jnp.exp(masked - newest[..., None]), 0.0)
        correct = jnp.exp(largest - newest)
        totals = totals * correct + jnp.sum(weight, axis=-1)
        accum = accum * correct[..., None] + jnp.einsum(
            "grtm,mgd->grtd", weight.astype(bf16), value_block, preferred_element_type=f32
        )
        return (newest, totals, accum), None

    start = (jnp.full(shape, -1e30, f32), jnp.zeros(shape, f32), jnp.zeros(shape + (HD,), f32))
    (_, totals, accum), _ = lax.scan(
        visit, start, (key_blocks, value_blocks, jnp.arange(count // width, dtype=jnp.int32))
    )
    attended = accum / totals[..., None]
    return jnp.transpose(attended, (2, 0, 1, 3)).reshape(tokens_here, AH * HD).astype(bf16)


def on_device(
    x_in,
    z_in,
    bc_in,
    dt_raw,
    a_log,
    dt_bias,
    d_skip,
    conv_x,
    conv_bc,
    norm_gain,
    seg_ids,
    query,
    keys,
    values,
):
    ranks = lax.axis_size("ctx")
    rows, width = x_in.shape[1:]
    share = BLK // rows
    blocks = ranks // share
    piece = width // share
    chunk = piece // CHUNKS
    reach = -(-(rows * ranks // 2 - 1) // rows)
    shape = jax.ShapeDtypeStruct
    state_type = bf16 if blocks <= 2 else f32

    wide = 4 * LANES
    packed = call(
        functools.partial(pack_body, share),
        [shape((rows, chunk + 3 * LANES), bf16)] * share
        + [shape((share, rows, chunk), bf16)]
        + [shape((rows + 16, wide), bf16)]
        + [shape((rows + 32, wide), bf16)] * 2,
        scratch=[
            pltpu.VMEM((rows, LANES), bf16),
            pltpu.VMEM((rows, bc_in.shape[2]), bf16),
            pltpu.VMEM((share, rows, chunk), bf16),
            pltpu.VMEM((share, rows, chunk), bf16),
            pltpu.VMEM((rows, wide), bf16),
            pltpu.VMEM((share, rows, 3 * LANES), bf16),
            pltpu.VMEM((16, wide), bf16),
            pltpu.VMEM((32, wide), bf16),
            pltpu.VMEM((32, wide), bf16),
            pltpu.VMEM((16, width), bf16),
            pltpu.SemaphoreType.DMA((5 * share + 11,)),
        ],
        in_specs=[hbm()] * 3 + [vmem()] + [hbm()] * 2,
        out_specs=[hbm()] * (share + 4),
        room=PACK_ROOM,
        bytes_accessed=5 * 2**20,
    )(x_in[0], bc_in[0], dt_raw[0], seg_ids, keys[0], values[0])
    send, send_b, (kv_own, kv_near, kv_far) = packed[:share], packed[share], packed[share + 1 :]
    order = [2, 3, 1]

    def exchanged(values):
        here = {0: values[0]}
        for m in order:
            here[m] = crossed(values[m], "ctx", m)
        return [here[m] for m in range(share)]

    pieces = exchanged(send)
    near, far = turned_on(kv_near, "ctx", 2), turned_on(kv_far, "ctx", 4)
    send_b, pieces[2] = lax.optimization_barrier((send_b, pieces[2]))
    groups = [[b * share + i for i in range(share)] for b in range(blocks)]
    pieces_b = lax.all_to_all(send_b, "ctx", 0, 0, tiled=True, axis_index_groups=groups)
    halo = []
    if blocks > 2:
        mine = jnp.concatenate([kv_own, near, far], axis=0)
        other = crossed(mine, "ctx", 1)
        halo = [mine, other]
    per_token = shape((BLK, LANES), f32)
    head_gains = jnp.concatenate([dt_bias, a_log, d_skip], axis=0)
    xc_a, bcc_first, state_a, ids_col, writes, *decay = call(
        functools.partial(first_body, share, blocks > 2),
        [
            shape((BLK, chunk), bf16),
            shape((BLK, 2 * LANES), bf16),
            shape((LANES, chunk), state_type),
            shape((BLK + 8, LANES), f32),
            shape((BLK, LANES), bf16),
        ]
        + ([shape((8, LANES), f32)] if blocks > 2 else []),
        scratch=[
            pltpu.VMEM((BLK + 8, chunk), f32),
            pltpu.VMEM((BLK + 8, wide), f32),
            pltpu.VMEM((3, BLK, LANES), f32),
        ],
        flops=0,
        bytes_accessed=1024,
    )(*pieces, conv_x[0], conv_bc[0], head_gains, *halo)
    bcc_mixing = bcc_first
    if blocks <= 2:
        near, far, bcc_mixing = lax.optimization_barrier((near, far, bcc_first))
        mine = jnp.concatenate([kv_own, near, far], axis=0)
        other = crossed(mine, "ctx", 1)
    xc_b, state_b = call(
        functools.partial(second_body, share, blocks > 2),
        [shape((BLK, chunk), bf16), shape((LANES, chunk), state_type)],
        scratch=[pltpu.VMEM((BLK + 8, chunk), f32), pltpu.VMEM((3, BLK, LANES), f32)],
        flops=2**28,
        bytes_accessed=3 * 2**20,
    )(pieces_b, conv_x[0], bcc_first, ids_col, writes, *halo)
    per_head = chunk // HD

    def entering(state, first):
        if blocks > 2:
            same = ids_col[BLK + 7, :] == ids_col[7, :]
            fade = jnp.where(same, decay[0][0, :], 0.0)[first : first + per_head]
            fade = jnp.repeat(fade, HD)[None, :]
            far = 1
            while far < blocks:
                came = shifted(state, "ctx", far * share)
                came_fade = shifted(fade, "ctx", far * share)
                state = state + fade * came
                fade = fade * came_fade
                far *= 2
        return turned_on(state, "ctx", share).astype(bf16)

    entry_a = entering(state_a, 0)
    entry_b = entering(state_b, per_head)

    local_a, local_b, bcc, keep = call(
        functools.partial(mixing_body, share),
        [shape((BLK, chunk), f32)] * CHUNKS + [shape((BLK, 2 * LANES), bf16), per_token],
        scratch=[
            pltpu.VMEM((24, piece + wide), f32),
            pltpu.VMEM((24, LANES), f32),
            pltpu.VMEM((3, 16, LANES), f32),
            pltpu.VMEM((16, piece), bf16),
        ],
        flops=2**31,
        bytes_accessed=4 * 2**20,
    )(*pieces, pieces_b, xc_a, xc_b, mine, other, conv_x[0], conv_bc[0], bcc_mixing, head_gains)

    if reach <= share:
        attended = call(
            attention_body,
            shape((rows, AH * HD), bf16),
            flops=2**30,
            bytes_accessed=2**20,
        )(query[0], mine, other)
    else:
        attended = gathered_attention(query[0], keys[0], values[0], seg_ids[0])
    local_a, attended = lax.optimization_barrier((local_a, attended))
    handoff = turned_on(attended, "pipe", 1)

    sent = []
    for c, (entry, local) in enumerate(((entry_a, local_a), (entry_b, local_b))):
        y = call(
            functools.partial(finish_body, share, c * per_head),
            [shape((share, rows, chunk), bf16)] if WHOLE[c] else [shape((rows, chunk), bf16)] * share,
            scratch=[pltpu.VMEM((BLK, chunk), f32)],
            flops=2**28,
            bytes_accessed=2 * 2**20,
        )(entry, bcc, keep, local)
        if WHOLE[c]:
            groups = [[b * share + i for i in range(share)] for b in range(blocks)]
            sent.append(
                lax.all_to_all(y[0], "ctx", 0, 0, tiled=True, axis_index_groups=groups)
            )
            continue
        sent += exchanged(y)
    mamba_out, handoff = call(
        functools.partial(norm_body, share),
        [shape((rows, width), bf16), shape((rows, AH * HD), bf16)],
        scratch=[pltpu.VMEM((share, rows, piece), bf16), pltpu.SemaphoreType.DMA((share + 1,))],
        out_specs=[hbm()] * 2,
        bytes_accessed=3 * 2**20,
    )(*sent, z_in[0], norm_gain, handoff)
    return (mamba_out[None], handoff[None])


def solution(mesh):
    in_specs = (
        P("pipe", "ctx", None),
        P("pipe", "ctx", None),
        P("pipe", "ctx", None),
        P("pipe", "ctx", None),
        P("pipe", None),
        P("pipe", None),
        P("pipe", None),
        P("pipe", None, None),
        P("pipe", None, None),
        P("pipe", None),
        P("pipe", "ctx"),
        P("pipe", "ctx", None),
        P("pipe", "ctx", None),
        P("pipe", "ctx", None),
    )
    out_specs = (P("pipe", "ctx", None), P("pipe", "ctx", None))
    return jax.shard_map(
        on_device, mesh=mesh, in_specs=in_specs, out_specs=out_specs, check_vma=False
    )
```

```python
import functools
import math

import jax
import jax.numpy as jnp
from jax import lax
from jax.experimental import pallas as pl
from jax.experimental.pallas import tpu as pltpu
from jax.sharding import PartitionSpec as P

G = 4
AH = 32
KVH = 4
HD = 64
BLK = 256
LANES = 128
LOCAL_HEADS = 32
CHUNKS = 2
PACK_ROOM = 58
WHOLE = (False, False)

norm_eps = 1e-05
bf16 = jnp.bfloat16
f32 = jnp.float32


def shifted(value, axis, steps):
    count = lax.axis_size(axis)
    return lax.ppermute(value, axis, [(i, i + steps) for i in range(count - steps)])


def turned_on(value, axis, steps):
    count = lax.axis_size(axis)
    return lax.ppermute(value, axis, [(i, (i + steps) % count) for i in range(count)])


def crossed(value, axis, mask):
    count = lax.axis_size(axis)
    return lax.ppermute(value, axis, [(i, i ^ mask) for i in range(count)])


def iota(shape, dim):
    return lax.broadcasted_iota(jnp.int32, shape, dim)


def call(body, outs, scratch=(), flops=0, bytes_accessed=0, room=48, **specs):
    return pl.pallas_call(
        body,
        out_shape=outs,
        scratch_shapes=list(scratch),
        compiler_params=pltpu.CompilerParams(vmem_limit_bytes=int(room * 2**20)),
        cost_estimate=pl.CostEstimate(
            flops=flops, bytes_accessed=bytes_accessed, transcendentals=0
        ),
        **specs,
    )


def hbm():
    return pl.BlockSpec(memory_space=pltpu.HBM)


def vmem():
    return pl.BlockSpec(memory_space=pltpu.VMEM)


def pack_body(share, x_hbm, bc_hbm, dt_hbm, ids_ref, k_hbm, v_hbm, *refs):
    sends, seconds = refs[:share], refs[share]
    kvs, rest = refs[share + 1 : share + 4], refs[share + 4 :]
    dt_ref, bc_ref, x_firsts, x_seconds, kv_ref, marks, own_extra, near_extra, far_extra = rest[:-2]
    x_tail, sems = rest[-2:]
    extras = (own_extra, near_extra, far_extra)
    me = lax.rem(lax.axis_index("ctx"), share)
    rows, width = x_hbm.shape
    piece = width // share
    chunk = piece // CHUNKS
    states = bc_hbm.shape[1] // (2 * G)
    wide = 4 * LANES
    started = []

    def start(source, target):
        copy = pltpu.make_async_copy(source, target, sems.at[len(started)])
        copy.start()
        started.append(copy)
        return copy

    order = (2, 3, 1, 0)
    steps_in, small_in = start(dt_hbm, dt_ref), start(bc_hbm, bc_ref)
    parts_in = []
    for c, held in enumerate((x_firsts, x_seconds)):
        for m in order:
            at = pl.multiple_of((me ^ m) * piece + c * chunk, LANES)
            if c == 0:
                parts_in.append(start(x_hbm.at[:, pl.ds(at, chunk)], held.at[m]))
            else:
                at = m * piece + chunk
                parts_in.append(start(x_hbm.at[:, pl.ds(at, chunk)], held.at[m]))
    kv_in = [
        start(source, kv_ref.at[:, pl.ds(side * wide // 2, wide // 2)])
        for side, source in enumerate((k_hbm, v_hbm))
    ]
    tail_in = start(x_hbm.at[pl.ds(rows - 16, 16), :], x_tail)
    arriving = len(started)
    number = ids_ref[...].astype(f32) + 1.0
    square = iota((rows, rows), 0) == iota((rows, rows), 1)
    column = jnp.sum(
        jnp.where(square, jnp.broadcast_to(number, (rows, rows)), 0.0), axis=1, keepdims=True
    )
    small = iota((rows, LANES), 1)
    steps_in.wait()
    steps = dt_ref[...].astype(f32)
    small_in.wait()
    for m in order:
        s = me ^ m
        turn = lax.rem(LANES - LOCAL_HEADS * s, LANES)
        marked = jnp.where(small < LOCAL_HEADS, pltpu.roll(steps, turn, 1), column).astype(bf16)
        for side in range(2):
            at = pl.multiple_of((side * G + s) * states, LANES)
            marks[m, :, side * states : (side + 1) * states] = bc_ref[:, pl.ds(at, states)]
        marks[m, :, 2 * states :] = marked
        start(marks.at[m], sends[m].at[:, pl.ds(chunk, 2 * states + LANES)])
    for i, m in enumerate(order):
        parts_in[i].wait()
        start(x_firsts.at[m], sends[m].at[:, pl.ds(0, chunk)])
    for i, m in enumerate(order):
        parts_in[share + i].wait()
        start(x_seconds.at[m], seconds.at[m])
    for copy in kv_in:
        copy.wait()
    for kv in kvs:
        start(kv_ref, kv.at[pl.ds(0, rows), :])
    lane = iota((rows, wide), 1)
    at = jnp.where(lane >= 3 * rows, lane - 3 * rows, lane)
    row = iota((rows, wide), 0)
    which = iota((16, wide), 0)
    tail_in.wait()
    bc_tail = bc_ref[rows - 16 :, :]
    for slot, extra in enumerate(extras):
        id_row = jnp.sum(jnp.where(at == row + rows * slot, column, 0.0), axis=0, keepdims=True)
        if slot == 0:
            extra[...] = jnp.where(which == 15, id_row, 0.0).astype(bf16)
        else:
            for part in range(2):
                s = 2 * (slot - 1) + part
                block = jnp.where(which == 15, id_row, 0.0)
                blocks = [
                    x_tail[:, s * piece + p * wide : s * piece + (p + 1) * wide].astype(f32)
                    for p in range(piece // wide)
                ]
                blocks.append(
                    jnp.concatenate(
                        [
                            bc_tail[:, s * states : (s + 1) * states].astype(f32),
                            bc_tail[:, (G + s) * states : (G + s + 1) * states].astype(f32),
                            jnp.broadcast_to(column[rows - 16 :, :], (16, 2 * LANES)),
                        ],
                        axis=1,
                    )
                )
                for i in range(3):
                    for p, source in enumerate(blocks):
                        block = jnp.where(which == 5 * i + p, source[13 + i : 14 + i, :], block)
                extra[16 * part : 16 * (part + 1), :] = block.astype(bf16)
        start(extra, kvs[slot].at[pl.ds(rows, extra.shape[0]), :])
    for copy in started[arriving:]:
        copy.wait()


def pick_halo(me, rows, mine, other):
    count = rows + 16
    second = count + rows
    third = second + rows + 32
    options = [
        other[second : second + 16, :],
        mine[second + 16 : second + 32, :],
        other[third : third + 16, :],
        mine[third + 16 : third + 32, :],
    ]
    picked = options[0].astype(f32)
    for j in range(1, 4):
        picked = jnp.where(me == j, options[j].astype(f32), picked)
    return jnp.where(lax.axis_index("ctx") >= 4, picked, 0.0)


def place_halo(scratch, picked, pieces):
    wide = picked.shape[1]
    for at, p in enumerate(pieces):
        which = iota((8, wide), 0)
        block = jnp.zeros((8, wide), f32)
        for i in range(3):
            block = jnp.where(which == 5 + i, picked[5 * i + p : 5 * i + p + 1, :], block)
        scratch[0:8, at * wide : (at + 1) * wide] = block


def conv_strip(src, columns, masks, taps):
    length = masks.shape[1]
    total = None
    for tap in range(4):
        term = taps[tap] * src[5 + tap : 5 + tap + length, columns]
        if tap < 3:
            term = term * masks[tap]
        total = term if total is None else total + term
    return (total * jax.nn.sigmoid(total)).astype(bf16)


def set_masks(masks, ids):
    length = masks.shape[1]
    own = ids[8 : 8 + length, :]
    for tap in range(3):
        masks[tap] = jnp.where(ids[5 + tap : 5 + tap + length, :] == own, 1.0, 0.0)


def taps_at(conv_ref, at):
    weights = conv_ref[:, pl.ds(pl.multiple_of(at, LANES), LANES)].astype(f32)
    return [weights[t : t + 1, :] for t in range(4)]


def one_hot(first, chunk):
    lane = iota((LANES, chunk), 0)
    head = iota((LANES, chunk), 1) // HD + first
    return jnp.where((lane % LOCAL_HEADS == head) & (lane < 3 * LOCAL_HEADS), 1.0, 0.0).astype(bf16)


def three_parts(value):
    lane = iota(value.shape, 1)
    high = value.astype(bf16).astype(f32)
    rest = value - high
    middle = rest.astype(bf16).astype(f32)
    low = rest - middle
    packed = jnp.where(
        lane < LOCAL_HEADS,
        high,
        jnp.where(
            lane < 2 * LOCAL_HEADS,
            pltpu.roll(middle, LOCAL_HEADS, 1),
            jnp.where(lane < 3 * LOCAL_HEADS, pltpu.roll(low, 2 * LOCAL_HEADS, 1), 0.0),
        ),
    )
    return packed.astype(bf16)


def conv_x_and_state(xs, masks, conv_ref, base, bcc, writes, first, xc_ref, state_ref):
    chunk = xc_ref.shape[1]
    for c in range(chunk // LANES):
        columns = slice(c * LANES, (c + 1) * LANES)
        xc_ref[:, columns] = conv_strip(xs, columns, masks, taps_at(conv_ref, base + c * LANES))
    factors = jnp.dot(writes, one_hot(first, chunk), preferred_element_type=f32)
    scaled = (xc_ref[...].astype(f32) * factors).astype(bf16)
    state = lax.dot_general(bcc, scaled, (((0,), (0,)), ((), ())), preferred_element_type=f32)
    state_ref[...] = state.astype(state_ref.dtype)


def turned(row, me):
    return pltpu.roll(
        jnp.broadcast_to(row, (8, LANES)), lax.rem(LANES - LOCAL_HEADS * me, LANES), 1
    )


def decays(marks, gains, me):
    length = marks.shape[0]
    raw = marks + turned(gains[0:1, :], me)[0:1, :]
    step = jnp.maximum(raw, 0.0) + jnp.log1p(jnp.exp(-jnp.abs(raw)))
    total = step * (-jnp.exp(turned(gains[1:2, :], me)[0:1, :]))
    row = iota((length, LANES), 0)
    reach = 1
    while reach < length:
        total = total + jnp.where(row >= reach, pltpu.roll(total, reach, 0), 0.0)
        reach *= 2
    return step, total


def first_body(share, with_halo, *refs):
    pieces = refs[:share]
    convx, convbc, gains = refs[share : share + 3]
    rest = refs[share + 3 :]
    me = lax.rem(lax.axis_index("ctx"), share)
    if with_halo:
        picked = pick_halo(me, pieces[0].shape[0], rest[0], rest[1])
        rest = rest[2:]
    xc_o, bcc_o, state_o, ids_o, writes_o, *decay_o, xs, bs, masks = rest
    chunk = xc_o.shape[1]
    piece = chunk * CHUNKS
    rows = pieces[0].shape[0]
    length = rows * share
    per_block = 4 * LANES
    if with_halo:
        place_halo(xs, picked, list(range(chunk // per_block)))
        place_halo(bs, picked, [4])
    else:
        xs[0:8, :] = jnp.zeros((8, chunk), f32)
        bs[0:8, :] = jnp.zeros((8, per_block), f32)
    for m in range(share):
        at = pl.multiple_of(8 + rows * (me ^ m), 8)
        xs[pl.ds(at, rows), :] = pieces[m][:, :chunk].astype(f32)
        bs[pl.ds(at, rows), : 3 * LANES] = pieces[m][:, chunk:].astype(f32)
    where_ids = 2 * LANES + LOCAL_HEADS
    ids_o[...] = jnp.broadcast_to(bs[:, where_ids : where_ids + 1], (length + 8, LANES))
    set_masks(masks, ids_o)
    for half in range(2):
        columns = slice(half * LANES, (half + 1) * LANES)
        taps = taps_at(convbc, half * G * LANES + me * LANES)
        bcc_o[:, columns] = conv_strip(bs, columns, masks, taps)
    step, total = decays(bs[8:, 2 * LANES : 3 * LANES], gains, me)
    own = ids_o[8:, :]
    last = length - 1
    writes = (
        jnp.where(own == own[last : last + 1, :], jnp.exp(total[last : last + 1, :] - total), 0.0)
        * step
    )
    for fade in decay_o:
        fade[...] = jnp.broadcast_to(jnp.exp(total[last : last + 1, :]), (8, LANES))
    packed = three_parts(writes)
    writes_o[...] = packed
    conv_x_and_state(xs, masks, convx, me * piece, bcc_o[:, :LANES], packed, 0, xc_o, state_o)


def second_body(share, with_halo, *refs):
    pieces = refs[0]
    convx, bcc, ids, writes = refs[1:5]
    rest = refs[5:]
    me = lax.rem(lax.axis_index("ctx"), share)
    if with_halo:
        picked = pick_halo(me, pieces.shape[1], rest[0], rest[1])
        rest = rest[2:]
    xc_o, state_o, xs, masks = rest
    chunk = xc_o.shape[1]
    rows = pieces.shape[1]
    blocks = chunk // (4 * LANES)
    if with_halo:
        place_halo(xs, picked, list(range(blocks, 2 * blocks)))
    else:
        xs[0:8, :] = jnp.zeros((8, chunk), f32)
    for i in range(share):
        xs[8 + rows * i : 8 + rows * (i + 1), :] = pieces[i].astype(f32)
    set_masks(masks, ids)
    base = me * (chunk * CHUNKS) + chunk
    conv_x_and_state(
        xs, masks, convx, base, bcc[:, :LANES], writes[...], chunk // HD, xc_o, state_o
    )


def mixing_body(share, *refs):
    pieces, seconds = refs[:share], refs[share]
    xcs, refs = refs[share + 1 : share + 1 + CHUNKS], refs[share + 1 + CHUNKS :]
    mine, other, convx, convbc, bcc_in, skip = refs[:6]
    rest = refs[6:]
    outs, (bcc, keep, head, head_ids, masks, first_x) = rest[:CHUNKS], rest[CHUNKS:]
    me = lax.rem(lax.axis_index("ctx"), share)
    length, chunk = xcs[0].shape
    rows = pieces[0].shape[0]
    piece = chunk * CHUNKS
    half = length // 2
    picked = pick_halo(me, rows, mine, other)
    place_halo(head, picked, list(range(5)))

    def first_rows(buffers, columns):
        start = buffers[0][:16, columns].astype(f32)
        for m in range(1, share):
            start = jnp.where(me == m, buffers[m][:16, columns].astype(f32), start)
        return start

    head[8:, :chunk] = first_rows(pieces, slice(0, chunk))
    head[8:, chunk:piece] = seconds[0, :16, :].astype(f32)
    head[8:, piece : piece + 3 * LANES] = first_rows(pieces, slice(chunk, chunk + 3 * LANES))
    where_ids = piece + 2 * LANES + LOCAL_HEADS
    head_ids[...] = jnp.broadcast_to(head[:, where_ids : where_ids + 1], (24, LANES))
    set_masks(masks, head_ids)
    for c in range(piece // LANES):
        columns = slice(c * LANES, (c + 1) * LANES)
        first_x[:, columns] = conv_strip(
            head, columns, masks, taps_at(convx, me * piece + c * LANES)
        )
    bcc[16:, :] = bcc_in[16:, :]
    for side in range(2):
        columns = slice(piece + side * LANES, piece + (side + 1) * LANES)
        taps = taps_at(convbc, side * G * LANES + me * LANES)
        bcc[:16, side * LANES : (side + 1) * LANES] = conv_strip(head, columns, masks, taps)

    inner = lax.dot_general(
        bcc[:, LANES:], bcc[:, :LANES], (((1,), (1,)), ((), ())), preferred_element_type=f32
    )
    ids = []
    for i in range(share):
        part = pieces[0][:, chunk + 2 * LANES :].astype(f32)
        for m in range(1, share):
            part = jnp.where((me ^ m) == i, pieces[m][:, chunk + 2 * LANES :].astype(f32), part)
        ids.append(part)
    ids = jnp.concatenate(ids, axis=0)
    across = ids.T[LOCAL_HEADS : LOCAL_HEADS + 1, :]
    own = jnp.broadcast_to(ids[:, LOCAL_HEADS : LOCAL_HEADS + 1], (length, length))
    allowed = (iota((length, length), 0) >= iota((length, length), 1)) & (own == across)
    inner = jnp.where(allowed, inner, 0.0)
    step, cums = decays(ids, skip, me)
    keep[...] = jnp.where(own[:, :LANES] == head_ids[7:8, :], jnp.exp(cums), 0.0)
    cum_rows = cums.T
    step_rows = step.T
    gains = three_parts(turned(skip[2:3, :], me))
    even = iota((half, LANES), 1) < HD
    for c in range(CHUNKS):
        first = c * (chunk // HD)
        spread = jnp.dot(gains, one_hot(first, chunk), preferred_element_type=f32)[0:1, :]
        for pair in range(chunk // LANES):
            columns = slice(pair * LANES, (pair + 1) * LANES)
            x_pair = jnp.concatenate(
                [
                    first_x[:, c * chunk + pair * LANES : c * chunk + (pair + 1) * LANES],
                    xcs[c][16:, columns],
                ],
                axis=0,
            )
            upper, lower = [], []
            for side in range(2):
                h = first + 2 * pair + side
                fade = cum_rows[h : h + 1, :]
                size = step_rows[h : h + 1, :]
                col = cums[:, h : h + 1]
                top = (
                    inner[:half, :half]
                    * (jnp.exp(jnp.minimum(col[:half] - fade[:, :half], 0.0)) * size[:, :half])
                ).astype(bf16)
                low = (
                    inner[half:, :] * (jnp.exp(jnp.minimum(col[half:] - fade, 0.0)) * size)
                ).astype(bf16)
                upper.append(jnp.dot(top, x_pair[:half, :], preferred_element_type=f32))
                lower.append(jnp.dot(low, x_pair, preferred_element_type=f32))
            gain = spread[:, columns]
            outs[c][:half, columns] = jnp.where(even, upper[0], upper[1]) + gain * x_pair[
                :half, :
            ].astype(f32)
            outs[c][half:, columns] = jnp.where(even, lower[0], lower[1]) + gain * x_pair[
                half:, :
            ].astype(f32)


def finish_body(share, first, state, bcc, keep, local, *rest):
    outs, total = rest[:-1], rest[-1]
    me = lax.rem(lax.axis_index("ctx"), share)
    chunk = local.shape[1]
    rows = outs[0].shape[-2]
    carried = jnp.dot(bcc[:, LANES:], state[...], preferred_element_type=f32)
    factors = jnp.dot(three_parts(keep[...]), one_hot(first, chunk), preferred_element_type=f32)
    total[...] = local[...] + carried * factors
    if len(outs) == 1:
        for i in range(share):
            outs[0][i] = total[rows * i : rows * (i + 1), :].astype(bf16)
        return
    for m in range(share):
        at = pl.multiple_of(rows * (me ^ m), rows)
        outs[m][...] = total[pl.ds(at, rows), :].astype(bf16)


def norm_body(share, *refs):
    z, gain, handed, out, handoff, buffer, sems = refs[-7:]
    me = lax.rem(lax.axis_index("ctx"), share)
    chunk = refs[0].shape[-1]
    parts, at = [], 0
    for whole in WHOLE:
        if whole:
            parts.append([lambda m, r=refs[at]: r[me ^ m]])
            at += 1
        else:
            parts.append([lambda m, r=refs[at : at + share]: r[m][...]])
            at += share
    piece = 2 * chunk
    copies = [pltpu.make_async_copy(handed, handoff, sems.at[share])]
    copies[0].start()
    for m in (0, 2, 3, 1):
        base = pl.multiple_of((me ^ m) * piece, LANES)
        gated = []
        for c, (source,) in enumerate(parts):
            gate = z[:, pl.ds(pl.multiple_of(base + c * chunk, LANES), chunk)].astype(f32)
            gated.append(source(m).astype(f32) * (gate * jax.nn.sigmoid(gate)))
        square = sum(jnp.sum(v * v, axis=1, keepdims=True) for v in gated)
        factor = lax.rsqrt(square / piece + norm_eps)
        for c, value in enumerate(gated):
            at = pl.ds(pl.multiple_of(base + c * chunk, LANES), chunk)
            buffer[m, :, c * chunk : (c + 1) * chunk] = (value * factor * gain[:, at]).astype(bf16)
        copies.append(
            pltpu.make_async_copy(buffer.at[m], out.at[:, pl.ds(base, piece)], sems.at[m])
        )
        copies[-1].start()
    for copy in copies:
        copy.wait()


def attention_body(q_ref, mine, other, out):
    rows = q_ref.shape[0]
    keys = 6 * rows
    ratio = AH // KVH
    heads_wide = KVH * HD
    here = lax.axis_index("ctx")
    odd = lax.rem(here, 2) == 1
    starts = (0, rows + 16, 2 * rows + 48)

    def id_rows(buffer):
        total = None
        for at in starts:
            row = buffer[at + rows : at + rows + 16, :].astype(f32)[15:16, :keys]
            total = row if total is None else total + row
        return total

    lane_row = iota((1, keys), 1)
    id_row = jnp.where(lane_row < 3 * rows, id_rows(mine), id_rows(other))
    own = mine[rows : rows + 16, :].astype(f32)[15:16, :rows]
    square = iota((rows, rows), 0) == iota((rows, rows), 1)
    column = jnp.sum(
        jnp.where(square, jnp.broadcast_to(own, (rows, rows)), 0.0), axis=1, keepdims=True
    )
    lane = iota((rows, keys), 1)
    earlier = (lane >= rows) | (lane <= iota((rows, keys), 0))
    sibling = (lane < 3 * rows) | (lane >= 4 * rows) | odd
    slot = lane % (3 * rows) // rows
    before = (slot == 0) | ((slot == 1) & (here >= 2)) | ((slot == 2) & (here >= 4))
    bias = jnp.where((id_row == column) & earlier & sibling & before, 0.0, -1e30)
    pairs = ratio // 2
    bias = jnp.concatenate([bias] * pairs, axis=0)
    even = iota((keys, LANES), 1) < HD
    even_out = iota((rows * pairs, LANES), 1) < HD

    def both(at, side):
        whole = jnp.concatenate(
            [b[s : s + rows, at : at + LANES] for b in (mine, other) for s in starts], axis=0
        ).astype(f32)
        kept = jnp.where(even == (side == 0), whole, 0.0)
        moved = pltpu.roll(kept, HD, 1)
        first, second = (kept, moved) if side == 0 else (moved, kept)
        return jnp.concatenate([first.astype(bf16), second.astype(bf16)], axis=0)

    for g in range(KVH):
        block = (g // 2) * LANES
        key_pair = both(block, g % 2)
        value_pair = both(heads_wide + block, g % 2)
        base = g * ratio * HD
        q = jnp.concatenate(
            [q_ref[:, base + i * LANES : base + (i + 1) * LANES] for i in range(pairs)], axis=0
        )
        scores = lax.dot_general(
            q, key_pair, (((1,), (1,)), ((), ())), preferred_element_type=f32
        ) * (1.0 / math.sqrt(HD))
        probs, totals = [], []
        for side in range(2):
            masked = scores[:, side * keys : (side + 1) * keys] + bias
            top = jnp.max(masked, axis=1, keepdims=True)
            weight = jnp.exp(masked - top)
            totals.append(jnp.sum(weight, axis=1, keepdims=True))
            probs.append(weight.astype(bf16))
        mixed = jnp.dot(
            jnp.concatenate(probs, axis=1), value_pair, preferred_element_type=f32
        ) / jnp.where(even_out, totals[0], totals[1])
        for i in range(pairs):
            out[:, base + i * LANES : base + (i + 1) * LANES] = mixed[
                i * rows : (i + 1) * rows, :
            ].astype(bf16)


def gathered_attention(query, keys, values, own_ids):
    tokens_here = query.shape[0]
    place = lax.axis_index("ctx")
    all_ids = lax.all_gather(own_ids, "ctx", axis=0, tiled=True)
    ratio = AH // KVH
    queries = query.reshape(tokens_here, KVH, ratio, HD)
    query_pos = place * tokens_here + jnp.arange(tokens_here)
    key_piece = lax.all_gather(keys, "ctx", axis=0, tiled=True)
    value_piece = lax.all_gather(values, "ctx", axis=0, tiled=True)
    count = key_piece.shape[0]
    width = math.gcd(count, 512)
    key_blocks = key_piece.reshape(count // width, width, KVH, HD)
    value_blocks = value_piece.reshape(count // width, width, KVH, HD)
    shape = (KVH, ratio, tokens_here)

    def visit(running, item):
        key_block, value_block, order = item
        first = order * width
        key_ids = lax.dynamic_slice_in_dim(all_ids, first, width)
        key_pos = first + jnp.arange(width)
        allowed = (query_pos[:, None] >= key_pos[None, :]) & (own_ids[:, None] == key_ids[None, :])
        largest, totals, accum = running
        logits = jnp.einsum(
            "tgrd,mgd->grtm", queries, key_block, preferred_element_type=f32
        ) / math.sqrt(HD)
        masked = jnp.where(allowed, logits, -1e30)
        newest = jnp.maximum(largest, jnp.max(masked, axis=-1))
        weight = jnp.where(allowed, jnp.exp(masked - newest[..., None]), 0.0)
        correct = jnp.exp(largest - newest)
        totals = totals * correct + jnp.sum(weight, axis=-1)
        accum = accum * correct[..., None] + jnp.einsum(
            "grtm,mgd->grtd", weight.astype(bf16), value_block, preferred_element_type=f32
        )
        return (newest, totals, accum), None

    start = (jnp.full(shape, -1e30, f32), jnp.zeros(shape, f32), jnp.zeros(shape + (HD,), f32))
    (_, totals, accum), _ = lax.scan(
        visit, start, (key_blocks, value_blocks, jnp.arange(count // width, dtype=jnp.int32))
    )
    attended = accum / totals[..., None]
    return jnp.transpose(attended, (2, 0, 1, 3)).reshape(tokens_here, AH * HD).astype(bf16)


def on_device(
    x_in,
    z_in,
    bc_in,
    dt_raw,
    a_log,
    dt_bias,
    d_skip,
    conv_x,
    conv_bc,
    norm_gain,
    seg_ids,
    query,
    keys,
    values,
):
    ranks = lax.axis_size("ctx")
    rows, width = x_in.shape[1:]
    share = BLK // rows
    blocks = ranks // share
    piece = width // share
    chunk = piece // CHUNKS
    reach = -(-(rows * ranks // 2 - 1) // rows)
    shape = jax.ShapeDtypeStruct
    state_type = bf16 if blocks <= 2 else f32

    wide = 4 * LANES
    packed = call(
        functools.partial(pack_body, share),
        [shape((rows, chunk + 3 * LANES), bf16)] * share
        + [shape((share, rows, chunk), bf16)]
        + [shape((rows + 16, wide), bf16)]
        + [shape((rows + 32, wide), bf16)] * 2,
        scratch=[
            pltpu.VMEM((rows, LANES), bf16),
            pltpu.VMEM((rows, bc_in.shape[2]), bf16),
            pltpu.VMEM((share, rows, chunk), bf16),
            pltpu.VMEM((share, rows, chunk), bf16),
            pltpu.VMEM((rows, wide), bf16),
            pltpu.VMEM((share, rows, 3 * LANES), bf16),
            pltpu.VMEM((16, wide), bf16),
            pltpu.VMEM((32, wide), bf16),
            pltpu.VMEM((32, wide), bf16),
            pltpu.VMEM((16, width), bf16),
            pltpu.SemaphoreType.DMA((5 * share + 11,)),
        ],
        in_specs=[hbm()] * 3 + [vmem()] + [hbm()] * 2,
        out_specs=[hbm()] * (share + 4),
        room=PACK_ROOM,
        bytes_accessed=5 * 2**20,
    )(x_in[0], bc_in[0], dt_raw[0], seg_ids, keys[0], values[0])
    send, send_b, (kv_own, kv_near, kv_far) = packed[:share], packed[share], packed[share + 1 :]
    order = [2, 3, 1]

    def exchanged(values):
        here = {0: values[0]}
        for m in order:
            here[m] = crossed(values[m], "ctx", m)
        return [here[m] for m in range(share)]

    pieces = exchanged(send)
    near, far = turned_on(kv_near, "ctx", 2), turned_on(kv_far, "ctx", 4)
    send_b, pieces[2] = lax.optimization_barrier((send_b, pieces[2]))
    groups = [[b * share + i for i in range(share)] for b in range(blocks)]
    pieces_b = lax.all_to_all(send_b, "ctx", 0, 0, tiled=True, axis_index_groups=groups)
    halo = []
    if blocks > 2:
        mine = jnp.concatenate([kv_own, near, far], axis=0)
        other = crossed(mine, "ctx", 1)
        halo = [mine, other]
    per_token = shape((BLK, LANES), f32)
    head_gains = jnp.concatenate([dt_bias, a_log, d_skip], axis=0)
    xc_a, bcc_first, state_a, ids_col, writes, *decay = call(
        functools.partial(first_body, share, blocks > 2),
        [
            shape((BLK, chunk), bf16),
            shape((BLK, 2 * LANES), bf16),
            shape((LANES, chunk), state_type),
            shape((BLK + 8, LANES), f32),
            shape((BLK, LANES), bf16),
        ]
        + ([shape((8, LANES), f32)] if blocks > 2 else []),
        scratch=[
            pltpu.VMEM((BLK + 8, chunk), f32),
            pltpu.VMEM((BLK + 8, wide), f32),
            pltpu.VMEM((3, BLK, LANES), f32),
        ],
        flops=0,
        bytes_accessed=1024,
    )(*pieces, conv_x[0], conv_bc[0], head_gains, *halo)
    bcc_mixing = bcc_first
    if blocks <= 2:
        near, far, bcc_mixing = lax.optimization_barrier((near, far, bcc_first))
        mine = jnp.concatenate([kv_own, near, far], axis=0)
        other = crossed(mine, "ctx", 1)
    xc_b, state_b = call(
        functools.partial(second_body, share, blocks > 2),
        [shape((BLK, chunk), bf16), shape((LANES, chunk), state_type)],
        scratch=[pltpu.VMEM((BLK + 8, chunk), f32), pltpu.VMEM((3, BLK, LANES), f32)],
        flops=2**28,
        bytes_accessed=3 * 2**20,
    )(pieces_b, conv_x[0], bcc_first, ids_col, writes, *halo)
    per_head = chunk // HD

    def entering(state, first, move):
        if blocks > 2:
            same = ids_col[BLK + 7, :] == ids_col[7, :]
            fade = jnp.where(same, decay[0][0, :], 0.0)[first : first + per_head]
            fade = jnp.repeat(fade, HD)[None, :]
            far = 1
            while far < blocks:
                came = shifted(state, "ctx", far * share)
                came_fade = shifted(fade, "ctx", far * share)
                state = state + fade * came
                fade = fade * came_fade
                far *= 2
        return move(state, "ctx", share).astype(bf16)

    entry_a = entering(state_a, 0, turned_on)
    entry_b = entering(state_b, per_head, shifted)

    local_a, local_b, bcc, keep = call(
        functools.partial(mixing_body, share),
        [shape((BLK, chunk), f32)] * CHUNKS + [shape((BLK, 2 * LANES), bf16), per_token],
        scratch=[
            pltpu.VMEM((24, piece + wide), f32),
            pltpu.VMEM((24, LANES), f32),
            pltpu.VMEM((3, 16, LANES), f32),
            pltpu.VMEM((16, piece), bf16),
        ],
        flops=2**31,
        bytes_accessed=4 * 2**20,
    )(*pieces, pieces_b, xc_a, xc_b, mine, other, conv_x[0], conv_bc[0], bcc_mixing, head_gains)

    if reach <= share:
        attended = call(
            attention_body,
            shape((rows, AH * HD), bf16),
            flops=2**30,
            bytes_accessed=2**20,
        )(query[0], mine, other)
    else:
        attended = gathered_attention(query[0], keys[0], values[0], seg_ids[0])
    local_a, attended = lax.optimization_barrier((local_a, attended))
    handoff = turned_on(attended, "pipe", 1)

    sent = []
    for c, (entry, local) in enumerate(((entry_a, local_a), (entry_b, local_b))):
        y = call(
            functools.partial(finish_body, share, c * per_head),
            [shape((share, rows, chunk), bf16)] if WHOLE[c] else [shape((rows, chunk), bf16)] * share,
            scratch=[pltpu.VMEM((BLK, chunk), f32)],
            flops=2**28,
            bytes_accessed=2 * 2**20,
        )(entry, bcc, keep, local)
        if WHOLE[c]:
            groups = [[b * share + i for i in range(share)] for b in range(blocks)]
            sent.append(
                lax.all_to_all(y[0], "ctx", 0, 0, tiled=True, axis_index_groups=groups)
            )
            continue
        sent += exchanged(y)
    mamba_out, handoff = call(
        functools.partial(norm_body, share),
        [shape((rows, width), bf16), shape((rows, AH * HD), bf16)],
        scratch=[pltpu.VMEM((share, rows, piece), bf16), pltpu.SemaphoreType.DMA((share + 1,))],
        out_specs=[hbm()] * 2,
        bytes_accessed=3 * 2**20,
    )(*sent, z_in[0], norm_gain, handoff)
    return (mamba_out[None], handoff[None])


def solution(mesh):
    in_specs = (
        P("pipe", "ctx", None),
        P("pipe", "ctx", None),
        P("pipe", "ctx", None),
        P("pipe", "ctx", None),
        P("pipe", None),
        P("pipe", None),
        P("pipe", None),
        P("pipe", None, None),
        P("pipe", None, None),
        P("pipe", None),
        P("pipe", "ctx"),
        P("pipe", "ctx", None),
        P("pipe", "ctx", None),
        P("pipe", "ctx", None),
    )
    out_specs = (P("pipe", "ctx", None), P("pipe", "ctx", None))
    return jax.shard_map(
        on_device, mesh=mesh, in_specs=in_specs, out_specs=out_specs, check_vma=False
    )
```
